256 devices in a mesh: mp: 32 (over z, y), tok: 8 (over x, core).
Axes of the slice: x: 4, y: 4, z: 8, core: 2. Of those that a mesh axis runs over, the one named last changes fastest.
Arguments:
- hidden: bfloat16 [2048, 32768], P('tok', 'mp'), may hold values from -6 to 6
- sign_bits: int32 [32768], P('mp'), may hold values from 0 to 1
- down_weight: int32 [32768, 16384], P('mp', 'tok'), may hold values from -127 to 127
- exponents: int32 [16384], P('tok'), may hold values from 12 to 14
- residual: bfloat16 [2048, 16384], P('mp', 'tok'), may hold values from -6 to 6
Outputs:
- updated: bfloat16 [2048, 16384], P('mp', 'tok')
The draws below stay inside these ranges and needn't reach their ends.
All inputs are finite; a program needn't handle non-finite values.
Results may differ from the reference program's by a relative error of at most 0.0046.
Values may be sent and summed in bfloat16 or wider, within the bound.
A program may use at most 128 MiB of HBM per device.

```python
import jax
import jax.numpy as jnp
from jax import lax

D = 16384
FF_DEV = 1024
FF = 32768
TOKENS = 2048
N_MP = 32
N_TOK = 8


def with_ends(entries, rng, low, largest):
    index_at = [jax.random.randint(jax.random.fold_in(rng, axis), (), 0, length) for axis, length in enumerate(entries.shape)]
    main_axis = entries.shape.index(max(entries.shape))
    next_to = index_at[:main_axis] + [(index_at[main_axis] + 1) % entries.shape[main_axis]] + index_at[main_axis + 1:]
    return entries.at[tuple(index_at)].set(low).at[tuple(next_to)].set(largest)


def levels(own_key, extent, split, smallest, largest):
    level, own = 1.0, jax.random.fold_in(own_key, 6)
    for position, shards_of in split:
        heights = jnp.exp(jax.random.uniform(jax.random.fold_in(own, position), (shards_of,), jnp.float32, smallest / len(split), largest / len(split)))
        level = level * jnp.repeat(heights, extent[position] // shards_of).reshape([-1 if axis == position else 1 for axis in range(len(extent))])
    return level


def normal_values(key, shape, deviation, most, shards=(), kind=jnp.bfloat16):
    factor_of = levels(key, shape, shards, -0.22, 0.18) if shards else 1.0
    entries = jax.random.normal(key, shape, jnp.float32) * deviation * factor_of
    return jnp.minimum(jnp.maximum(entries, -most), most).astype(kind)


def setup_inputs(seed: int = 0) -> dict:
    key_list = jax.random.split(jax.random.key(seed), 6)
    hidden = normal_values(key_list[0], (TOKENS, FF), 1.0, 6.0, ((0, 8), (1, 32)))
    sign_bits = with_ends(jax.random.randint(key_list[1], (FF,), 0, 2), jax.random.fold_in(key_list[1], 1), 0, 1).astype(jnp.int32)
    down_weight = with_ends(jax.random.randint(key_list[2], (FF, D), -127, 128), jax.random.fold_in(key_list[2], 1), -127, 127).astype(jnp.int32)
    exponents = with_ends(jax.random.randint(key_list[3], (D,), 5 + min(FF // 4, 1) + min(FF // 16, 1) + min(FF // 64, 1) + min(FF // 256, 1) + min(FF // 1024, 1) + min(FF // 4096, 1) + min(FF // 16384, 1) + min(FF // 65536, 1) + min(FF // 262144, 1), 8 + min(FF // 4, 1) + min(FF // 16, 1) + min(FF // 64, 1) + min(FF // 256, 1) + min(FF // 1024, 1) + min(FF // 4096, 1) + min(FF // 16384, 1) + min(FF // 65536, 1) + min(FF // 262144, 1)), jax.random.fold_in(key_list[3], 1), 5 + min(FF // 4, 1) + min(FF // 16, 1) + min(FF // 64, 1) + min(FF // 256, 1) + min(FF // 1024, 1) + min(FF // 4096, 1) + min(FF // 16384, 1) + min(FF // 65536, 1) + min(FF // 262144, 1), (8 + min(FF // 4, 1) + min(FF // 16, 1) + min(FF // 64, 1) + min(FF // 256, 1) + min(FF // 1024, 1) + min(FF // 4096, 1) + min(FF // 16384, 1) + min(FF // 65536, 1) + min(FF // 262144, 1)) - 1).astype(jnp.int32)
    residual = normal_values(key_list[4], (TOKENS, D), 1.0, 6.0, ((0, 32), (1, 8)))
    return {"hidden": hidden, "sign_bits": sign_bits, "down_weight": down_weight, "exponents": exponents, "residual": residual}


def walsh_matrix(order):
    bit_total = order.bit_length() - 1
    left = lax.broadcasted_iota(jnp.int32, (order, order), 0)
    right = lax.broadcasted_iota(jnp.int32, (order, order), 1)
    parity = jnp.zeros((order, order), jnp.int32)
    for level in range(bit_total):
        parity = parity + ((left // (2 ** level)) % 2) * ((right // (2 ** level)) % 2)
    return (1 - 2 * (parity % 2)).astype(jnp.float32)


def reference(hidden, sign_bits, down_weight, exponents, residual):
    token_total = hidden.shape[0]
    ff_total = hidden.shape[1]
    flipped = hidden.astype(jnp.float32) * (2 * sign_bits - 1).astype(jnp.float32)
    blocks = flipped.reshape(token_total, N_MP, FF_DEV)
    crossed = jnp.einsum("rqj,pq->rpj", blocks, walsh_matrix(N_MP), precision=lax.Precision.HIGHEST)
    rotated_full = jnp.einsum("rpj,jk->rpk", crossed, walsh_matrix(FF_DEV), precision=lax.Precision.HIGHEST)
    rotated = (rotated_full.reshape(token_total, ff_total) * (1.0 / (ff_total ** 0.5))).astype(jnp.bfloat16)
    block_cols = D // N_TOK
    scales = jnp.exp2(-exponents.astype(jnp.float32))

    def one_block(block_index):
        first_col = (block_index * block_cols).astype(jnp.int32)
        weight_cols = lax.dynamic_slice_in_dim(down_weight, first_col, block_cols, 1).astype(jnp.bfloat16)
        scale_cols = lax.dynamic_slice_in_dim(scales, first_col, block_cols, 0)
        return jnp.dot(rotated, weight_cols, preferred_element_type=jnp.float32) * scale_cols

    pieces = lax.map(one_block, jnp.arange(N_TOK, dtype=jnp.int32))
    product = jnp.transpose(pieces, (1, 0, 2)).reshape(token_total, D)
    return (residual.astype(jnp.float32) + product).astype(jnp.bfloat16)
```

```python
import functools
import math

import jax
import jax.numpy as jnp
from jax import lax
from jax.experimental import pallas as pl
from jax.experimental.pallas import tpu as pltpu
from jax.sharding import PartitionSpec as P

MESH = pl.DeviceIdType.MESH
F32, BF16 = jnp.float32, jnp.bfloat16
NZ, NY, NX = 8, 4, 4
NMP = NZ * NY
UNITS = 1024
LANES = 128
COLS = 2048
YW = 1280
ZW = COLS - YW
YH, ZH = YW // 2, ZW // 2
ROWS = 64


def butterfly(v):
    count = v.shape[0]
    rest = v.shape[1:]
    span = 1
    while span < count:
        pairs = v.reshape((count // (2 * span), 2, span) + rest)
        low, high = pairs[:, 0], pairs[:, 1]
        v = jnp.stack([low + high, low - high], axis=1).reshape((count,) + rest)
        span *= 2
    return v


def walsh(order):
    both = lax.broadcasted_iota(jnp.int32, (order, order), 0) & lax.broadcasted_iota(
        jnp.int32, (order, order), 1
    )
    both = both ^ (both >> 4)
    both = both ^ (both >> 2)
    both = both ^ (both >> 1)
    return (1 - 2 * (both & 1)).astype(F32).astype(BF16)


def send(src, dst, send_sem, recv_sem, device):
    pltpu.make_async_remote_copy(
        src_ref=src,
        dst_ref=dst,
        send_sem=send_sem,
        recv_sem=recv_sem,
        device_id=device,
        device_id_type=MESH,
    ).start()


def drain(buf, sem):
    pltpu.make_async_copy(buf, buf, sem).wait()


def kernel(
    hid, sgn, w_hbm, expo, res, out,
    slab, recv1, mid, rot, recv2, act, w, w32, part,
    ys1, yr1, ys2, yr2, zs1, zr1, zs2, zr2, us1, ur1, us2, ur2, vs1, vr1, vs2, vr2,
    w_sem, a1_sem, a2_send, a2_recv, ag_send, ag_direct, ag_core,
    y_send, yr1_sem, yr2_sem, z_send, zr1_sem, zr2_sem,
    u_send, ur1_sem, ur2_sem, v_send, vr1_sem, vr2_sem,
):
    m, t = lax.axis_index("mp"), lax.axis_index("tok")
    z, y = lax.div(m, NY), lax.rem(m, NY)
    x, core = lax.div(t, 2), lax.rem(t, 2)

    def zmod(v):
        return lax.rem(v + NZ, NZ)

    def ymod(v):
        return lax.rem(v + NY, NY)

    def at_zy(zz, yy):
        return (zz * NY + yy, t)

    def at_x(xx, cc):
        return (m, xx * 2 + cc)

    sibling = at_x(x, 1 - core)
    y_next = (at_zy(z, ymod(y + 1)), at_zy(z, ymod(y - 1)))
    z_next = (at_zy(zmod(z + 1), y), at_zy(zmod(z - 1), y))

    barrier = pltpu.get_barrier_semaphore()

    def greet(i, _):
        pl.semaphore_signal(
            barrier, inc=1, device_id=(lax.rem(m + i, NMP), t), device_id_type=MESH
        )
        return 0

    lax.fori_loop(1, NMP, greet, 0)
    for dx in (1, 2, 3):
        pl.semaphore_signal(
            barrier, inc=1, device_id=at_x(lax.rem(x + dx, NX), core), device_id_type=MESH
        )
    pl.semaphore_signal(barrier, inc=1, device_id=sibling, device_id_type=MESH)

    w_rows = UNITS // 8
    for i in range(8):
        rows = pl.ds(i * w_rows, w_rows)
        pltpu.make_async_copy(w_hbm.at[rows], w32.at[rows], w_sem.at[i]).start()

    signs = (2 * sgn[...] - 1).astype(F32)

    def build(j, _):
        rows = hid[pl.ds(pl.multiple_of(j * 16, 16), 16), :].astype(F32) * signs
        for half in range(2):
            group = 2 * j + half
            dest = lax.rem(group, NZ) * NY + lax.div(group, NZ)
            own = rows[half * 8:half * 8 + 8]
            tall = jnp.concatenate(
                [own[:, k * LANES:(k + 1) * LANES] for k in range(8)], axis=0
            )
            slab[dest] = tall.astype(BF16)
        return 0

    lax.fori_loop(0, 16, build, 0)
    pl.semaphore_wait(barrier, NMP - 1 + 4)

    def spread(i, _):
        dest = lax.rem(m + i, NMP)
        send(slab.at[dest], recv1.at[m], a1_sem.at[0], a1_sem.at[1], (dest, t))
        return 0

    lax.fori_loop(1, NMP, spread, 0)
    recv1[m] = slab[m]

    def convert(j, _):
        rows = pl.ds(pl.multiple_of(j * 16, 16), 16)
        w[rows, :] = w32[rows, :].astype(F32).astype(BF16)
        return 0

    for i in range(8):
        rows = pl.ds(i * w_rows, w_rows)
        pltpu.make_async_copy(w_hbm.at[rows], w32.at[rows], w_sem.at[i]).wait()
        lax.fori_loop(i * w_rows // 16, (i + 1) * w_rows // 16, convert, 0)
    small_walsh = walsh(LANES)

    drain(recv1.at[pl.ds(0, NMP - 1)], a1_sem.at[1])

    def rotate_low(i, _):
        blocks = pl.ds(i * 4, 4)
        lanes = jnp.dot(
            recv1[blocks].reshape(256, LANES), small_walsh, preferred_element_type=F32
        ).reshape(4, 8, 8, LANES)
        for b in range(4):
            mid[i * 4 + b] = butterfly(lanes[b]).reshape(ROWS, LANES)
        return 0

    lax.fori_loop(0, 8, rotate_low, 0)
    inv_root = 1.0 / math.sqrt(NMP * UNITS)

    def rotate_high(i, _):
        rows = pl.ds(pl.multiple_of(i * 16, 16), 16)
        rot[:, rows, :] = (butterfly(mid[:, rows, :]) * inv_root).astype(BF16)
        return 0

    lax.fori_loop(0, 4, rotate_high, 0)

    def give_back(j, to_y, first):
        def one(i, _):
            to_z = lax.rem(z + i, NZ)
            dest = to_z * NY + to_y
            send(rot.at[dest], recv2.at[j, z], a2_send, a2_recv.at[j], (dest, t))
            return 0

        lax.fori_loop(first, NZ, one, 0)

    give_back(0, ymod(y + 2), 0)
    give_back(1, ymod(y - 1), 0)
    give_back(2, ymod(y + 1), 0)
    give_back(3, y, 1)
    recv2[3, z] = rot[m]

    def gather_own(j):
        count = NZ if j < 3 else NZ - 1
        drain(recv2.at[j, pl.ds(0, count)], a2_recv.at[j])

        def one(i, _):
            pieces = []
            for half in range(2):
                tall = recv2[j, 2 * i + half].astype(F32)
                pieces.append(
                    jnp.concatenate([tall[k * 8:k * 8 + 8] for k in range(8)], axis=1)
                )
            rows = pl.ds(pl.multiple_of(i * 16, 16), 16)
            act[j, t, rows, :] = jnp.concatenate(pieces, axis=0).astype(BF16)
            return 0

        lax.fori_loop(0, 4, one, 0)
        mine = act.at[j, t]
        for i, dx in enumerate((1, 3, 2)):
            send(mine, mine, ag_send.at[j], ag_direct.at[j, i], at_x(lax.rem(x + dx, NX), core))
        send(mine, mine, ag_send.at[j], ag_core.at[j], sibling)

    def pass_on(j):
        for i, dx in enumerate((1, 3, 2)):
            piece = act.at[j, lax.rem(x - dx + NX, NX) * 2 + core]
            drain(piece, ag_direct.at[j, i])
            send(piece, piece, ag_send.at[j], ag_core.at[j], sibling)

    def multiply(j):
        drain(act.at[j, pl.ds(0, 4)], ag_core.at[j])

        def one(i, _):
            cols = pl.ds(pl.multiple_of(i * 256, 256), 256)
            part[j, :, :, cols] = jnp.dot(
                act[j].reshape(NZ * ROWS, UNITS), w[:, cols], preferred_element_type=F32
            ).reshape(NZ, ROWS, 256)
            return 0

        lax.fori_loop(0, COLS // 256, one, 0)

    def compose(d, step, j, zz, low, half, incoming, dst):
        this, other = d * half, (1 - d) * half
        if step == 1:
            dst[...] = part[j, zz, :, pl.ds(low + this, half)].astype(BF16)
        elif step == 2:
            dst[:, pl.ds(this, half)] = (
                part[j, zz, :, pl.ds(low + this, half)] + incoming[...].astype(F32)
            ).astype(BF16)
            dst[:, pl.ds(other, half)] = part[j, zz, :, pl.ds(low + other, half)].astype(BF16)
        else:
            dst[...] = (
                part[j, zz, :, pl.ds(low, 2 * half)] + incoming[...].astype(F32)
            ).astype(BF16)

    def z_target(d, step):
        return zmod(z + (5 - step) * (1 - 2 * d))

    def z_hop(j, step, low, half, s1, r1, s2, r2, s_sem, r1_sem, r2_sem):
        for d in range(2):
            zz = z_target(d, step)
            if step == 1:
                compose(d, 1, j, zz, low, half, None, s1.at[d])
                send(s1.at[d], r1.at[d], s_sem.at[0], r1_sem.at[d], z_next[d])
                continue
            if step == 2:
                incoming, sem = r1.at[d], r1_sem.at[d]
            else:
                incoming, sem = r2.at[d, step - 3], r2_sem.at[d, step - 3]
            drain(incoming, sem)
            compose(d, step, j, zz, low, half, incoming, s2.at[d, step - 2])
            send(
                s2.at[d, step - 2], r2.at[d, step - 2],
                s_sem.at[1], r2_sem.at[d, step - 2], z_next[d],
            )

    def z_first(j, step):
        z_hop(
            j, step, YW, ZH, zs1.at[j], zr1.at[j], zs2.at[j], zr2.at[j],
            z_send, zr1_sem.at[j], zr2_sem.at[j],
        )

    def z_first_end(j):
        for d in range(2):
            drain(zr2.at[j, d, 2], zr2_sem.at[j, d, 2])
        part[j, z, :, pl.ds(YW, ZW)] = (
            part[j, z, :, pl.ds(YW, ZW)] + zr2[j, 0, 2].astype(F32) + zr2[j, 1, 2].astype(F32)
        )

    def z_second(step):
        z_hop(3, step, 0, YH, us1, ur1, us2, ur2, u_send, ur1_sem, ur2_sem)

    def block_at(k):
        up = lax.div(k + 1, 2)
        return zmod(z + 4 + up * (1 - 2 * lax.rem(k + 1, 2)))

    def y_first_start(k, _):
        zz = block_at(k)
        for d in range(2):
            compose(d, 1, 0, zz, 0, YH, None, ys1.at[d, k])
            send(ys1.at[d, k], yr1.at[d, k], y_send.at[0], yr1_sem.at[d, k], y_next[d])
        return 0

    def y_first_pass(d):
        def one(k, _):
            zz = block_at(k)
            drain(yr1.at[d, k], yr1_sem.at[d, k])
            compose(d, 2, 1 + d, zz, 0, YH, yr1.at[d, k], ys2.at[d, k])
            send(ys2.at[d, k], yr2.at[d, k], y_send.at[1], yr2_sem.at[d, k], y_next[d])
            return 0

        return one

    def y_first_both(k, _):
        y_first_pass(0)(k, 0)
        y_first_pass(1)(k, 0)
        return 0

    def y_first_end(k, _):
        zz = block_at(k)
        for d in range(2):
            drain(yr2.at[d, k], yr2_sem.at[d, k])
        part[3, zz, :, pl.ds(0, YW)] = (
            part[3, zz, :, pl.ds(0, YW)] + yr2[0, k].astype(F32) + yr2[1, k].astype(F32)
        )
        return 0

    def y_second_start():
        for d in range(2):
            compose(d, 1, 0, z, YW, ZH, None, vs1.at[d])
            send(vs1.at[d], vr1.at[d], v_send.at[0], vr1_sem.at[d], y_next[d])

    def y_second_pass(d):
        drain(vr1.at[d], vr1_sem.at[d])
        compose(d, 2, 1 + d, z, YW, ZH, vr1.at[d], vs2.at[d])
        send(vs2.at[d], vr2.at[d], v_send.at[1], vr2_sem.at[d], y_next[d])

    gather_own(0)
    gather_own(1)
    pass_on(0)
    gather_own(2)
    gather_own(3)
    multiply(0)
    z_first(0, 1)
    lax.fori_loop(0, 8, y_first_start, 0)
    pass_on(1)
    multiply(1)
    z_first(1, 1)
    z_first(0, 2)
    lax.fori_loop(0, 2, y_first_pass(0), 0)
    pass_on(2)
    multiply(2)
    z_first(2, 1)
    z_first(1, 2)
    z_first(0, 3)
    lax.fori_loop(0, 2, y_first_pass(1), 0)
    lax.fori_loop(2, 4, y_first_both, 0)
    pass_on(3)
    multiply(3)
    z_first(3, 1)
    z_first(2, 2)
    z_first(1, 3)
    z_first(0, 4)
    lax.fori_loop(4, 8, y_first_both, 0)
    z_first(3, 2)
    z_first(2, 3)
    z_first(1, 4)
    z_first_end(0)
    y_second_start()
    lax.fori_loop(0, 1, y_first_end, 0)
    z_second(1)
    z_first(3, 3)
    z_first(2, 4)
    z_first_end(1)
    y_second_pass(0)
    lax.fori_loop(1, 3, y_first_end, 0)
    z_second(2)
    z_first(3, 4)
    z_first_end(2)
    y_second_pass(1)
    lax.fori_loop(3, 5, y_first_end, 0)
    z_second(3)
    z_first_end(3)
    lax.fori_loop(5, 7, y_first_end, 0)
    z_second(4)
    lax.fori_loop(7, 8, y_first_end, 0)

    scales = jnp.exp2(-expo[...].astype(F32))
    for d in range(2):
        drain(vr2.at[d], vr2_sem.at[d])
    total = part[3, z, :, pl.ds(YW, ZW)] + vr2[0].astype(F32) + vr2[1].astype(F32)
    out[:, YW:] = (res[:, YW:].astype(F32) + total * scales[:, YW:]).astype(BF16)
    for d in range(2):
        drain(ur2.at[d, 2], ur2_sem.at[d, 2])
    total = part[3, z, :, pl.ds(0, YW)] + ur2[0, 2].astype(F32) + ur2[1, 2].astype(F32)
    out[:, :YW] = (res[:, :YW].astype(F32) + total * scales[:, :YW]).astype(BF16)

    drain(slab.at[pl.ds(0, NMP - 1)], a1_sem.at[0])
    drain(rot.at[pl.ds(0, NMP - 1)], a2_send)
    for j in range(4):
        drain(act.at[j, pl.ds(0, 7)], ag_send.at[j])
    for buf, sem in (
        (ys1, y_send.at[0]), (ys2, y_send.at[1]), (zs1, z_send.at[0]), (zs2, z_send.at[1]),
        (us1, u_send.at[0]), (us2, u_send.at[1]), (vs1, v_send.at[0]), (vs2, v_send.at[1]),
    ):
        drain(buf, sem)


def per_device(hidden, sign_bits, down_weight, exponents, residual):
    vmem = pl.BlockSpec(memory_space=pltpu.VMEM)

    def pair(*shape):
        return [pltpu.VMEM(shape, BF16)] * 2

    dma = pltpu.SemaphoreType.DMA
    return pl.pallas_call(
        kernel,
        out_shape=jax.ShapeDtypeStruct((ROWS, COLS), BF16),
        in_specs=[vmem, vmem, pl.BlockSpec(memory_space=pl.ANY), vmem, vmem],
        out_specs=vmem,
        scratch_shapes=[
            pltpu.VMEM((NMP, ROWS, LANES), BF16),
            pltpu.VMEM((NMP, ROWS, LANES), BF16),
            pltpu.VMEM((NMP, ROWS, LANES), F32),
            pltpu.VMEM((NMP, ROWS, LANES), BF16),
            pltpu.VMEM((4, NZ, ROWS, LANES), BF16),
            pltpu.VMEM((4, NZ, ROWS, UNITS), BF16),
            pltpu.VMEM((UNITS, COLS), BF16),
            pltpu.VMEM((UNITS, COLS), jnp.int32),
            pltpu.VMEM((4, NZ, ROWS, COLS), F32),
            *pair(2, 8, ROWS, YH),
            *pair(2, 8, ROWS, YW),
            *pair(4, 2, ROWS, ZH),
            *pair(4, 2, 3, ROWS, ZW),
            *pair(2, ROWS, YH),
            *pair(2, 3, ROWS, YW),
            *pair(2, ROWS, ZH),
            *pair(2, ROWS, ZW),
            dma((8,)), dma((2,)), dma, dma((4,)), dma((4,)), dma((4, 3)), dma((4,)),
            dma((2,)), dma((2, 8)), dma((2, 8)), dma((2,)), dma((4, 2)), dma((4, 2, 3)),
            dma((2,)), dma((2,)), dma((2, 3)), dma((2,)), dma((2,)), dma((2,)),
        ],
        compiler_params=pltpu.CompilerParams(
            collective_id=0, has_side_effects=True, vmem_limit_bytes=60 * 2**20
        ),
        cost_estimate=pl.CostEstimate(
            flops=2 * 2048 * UNITS * COLS, bytes_accessed=10 * 2**20, transcendentals=0
        ),
    )(
        hidden,
        sign_bits.reshape(1, UNITS),
        down_weight,
        exponents.reshape(1, COLS),
        residual,
    )


def solution(mesh):
    return jax.shard_map(
        per_device,
        mesh=mesh,
        in_specs=(P("tok", "mp"), P("mp"), P("mp", "tok"), P("tok"), P("mp", "tok")),
        out_specs=P("mp", "tok"),
        check_vma=False,
    )
```

```python
import functools
import math

import jax
import jax.numpy as jnp
from jax import lax
from jax.experimental import pallas as pl
from jax.experimental.pallas import tpu as pltpu
from jax.sharding import PartitionSpec as P

MESH = pl.DeviceIdType.MESH
F32, BF16 = jnp.float32, jnp.bfloat16
NZ, NY, NX = 8, 4, 4
NMP = NZ * NY
UNITS = 1024
LANES = 128
COLS = 2048
Y_CUT = (640, 640)
Z_CUT = (384, 384)
YW, ZW = sum(Y_CUT), sum(Z_CUT)
ROWS = 64


def butterfly(v):
    count = v.shape[0]
    rest = v.shape[1:]
    span = 1
    while span < count:
        pairs = v.reshape((count // (2 * span), 2, span) + rest)
        low, high = pairs[:, 0], pairs[:, 1]
        v = jnp.stack([low + high, low - high], axis=1).reshape((count,) + rest)
        span *= 2
    return v


def walsh(order):
    both = lax.broadcasted_iota(jnp.int32, (order, order), 0) & lax.broadcasted_iota(
        jnp.int32, (order, order), 1
    )
    both = both ^ (both >> 4)
    both = both ^ (both >> 2)
    both = both ^ (both >> 1)
    return (1 - 2 * (both & 1)).astype(F32).astype(BF16)


def send(src, dst, send_sem, recv_sem, device):
    pltpu.make_async_remote_copy(
        src_ref=src,
        dst_ref=dst,
        send_sem=send_sem,
        recv_sem=recv_sem,
        device_id=device,
        device_id_type=MESH,
    ).start()


def drain(buf, sem):
    pltpu.make_async_copy(buf, buf, sem).wait()


def kernel(
    hid, sgn, w_hbm, expo, res, out,
    slab, recv1, mid, rot, recv2, act, w, w32, part,
    ys1a, ys1b, yr1a, yr1b, ys2, yr2, zs1a, zs1b, zr1a, zr1b, zs2, zr2,
    us1a, us1b, ur1a, ur1b, us2, ur2, vs1a, vs1b, vr1a, vr1b, vs2, vr2,
    w_sem, a1_sem, a2_send, a2_recv, ag_send, ag_direct, ag_core,
    y_send, yr1_sem, yr2_sem, z_send, zr1_sem, zr2_sem,
    u_send, ur1_sem, ur2_sem, v_send, vr1_sem, vr2_sem,
):
    ys1, yr1, zs1, zr1 = (ys1a, ys1b), (yr1a, yr1b), (zs1a, zs1b), (zr1a, zr1b)
    us1, ur1, vs1, vr1 = (us1a, us1b), (ur1a, ur1b), (vs1a, vs1b), (vr1a, vr1b)
    m, t = lax.axis_index("mp"), lax.axis_index("tok")
    z, y = lax.div(m, NY), lax.rem(m, NY)
    x, core = lax.div(t, 2), lax.rem(t, 2)

    def zmod(v):
        return lax.rem(v + NZ, NZ)

    def ymod(v):
        return lax.rem(v + NY, NY)

    def at_zy(zz, yy):
        return (zz * NY + yy, t)

    def at_x(xx, cc):
        return (m, xx * 2 + cc)

    sibling = at_x(x, 1 - core)
    y_next = (at_zy(z, ymod(y + 1)), at_zy(z, ymod(y - 1)))
    z_next = (at_zy(zmod(z + 1), y), at_zy(zmod(z - 1), y))

    barrier = pltpu.get_barrier_semaphore()

    def far_first(i):
        offset = NMP // 2 + lax.div(i + 1, 2) * (1 - 2 * lax.rem(i, 2))
        return lax.rem(m + offset, NMP)

    def greet(i, _):
        pl.semaphore_signal(barrier, inc=1, device_id=(far_first(i), t), device_id_type=MESH)
        return 0

    lax.fori_loop(0, NMP - 1, greet, 0)
    for dx in (1, 2, 3):
        pl.semaphore_signal(
            barrier, inc=1, device_id=at_x(lax.rem(x + dx, NX), core), device_id_type=MESH
        )
    pl.semaphore_signal(barrier, inc=1, device_id=sibling, device_id_type=MESH)

    w_rows = UNITS // 8
    for i in range(8):
        rows = pl.ds(i * w_rows, w_rows)
        pltpu.make_async_copy(w_hbm.at[rows], w32.at[rows], w_sem.at[i]).start()

    signs = (2 * sgn[...] - 1).astype(F32)

    def build(j, _):
        rows = hid[pl.ds(pl.multiple_of(j * 16, 16), 16), :].astype(F32) * signs
        for half in range(2):
            group = 2 * j + half
            dest = lax.rem(group, NZ) * NY + lax.div(group, NZ)
            own = rows[half * 8:half * 8 + 8]
            tall = jnp.concatenate(
                [own[:, k * LANES:(k + 1) * LANES] for k in range(8)], axis=0
            )
            slab[dest] = tall.astype(BF16)
        return 0

    lax.fori_loop(0, 16, build, 0)
    pl.semaphore_wait(barrier, NMP - 1 + 4)

    def spread(i, _):
        dest = far_first(i)
        send(slab.at[dest], recv1.at[m], a1_sem.at[0], a1_sem.at[1], (dest, t))
        return 0

    lax.fori_loop(0, NMP - 1, spread, 0)
    recv1[m] = slab[m]

    def convert(j, _):
        rows = pl.ds(pl.multiple_of(j * 16, 16), 16)
        w[rows, :] = w32[rows, :].astype(F32).astype(BF16)
        return 0

    for i in range(8):
        rows = pl.ds(i * w_rows, w_rows)
        pltpu.make_async_copy(w_hbm.at[rows], w32.at[rows], w_sem.at[i]).wait()
        lax.fori_loop(i * w_rows // 16, (i + 1) * w_rows // 16, convert, 0)
    small_walsh = walsh(LANES)

    drain(recv1.at[pl.ds(0, NMP - 1)], a1_sem.at[1])

    def rotate_low(i, _):
        blocks = pl.ds(i * 4, 4)
        lanes = jnp.dot(
            recv1[blocks].reshape(256, LANES), small_walsh, preferred_element_type=F32
        ).reshape(4, 8, 8, LANES)
        for b in range(4):
            mid[i * 4 + b] = butterfly(lanes[b]).reshape(ROWS, LANES)
        return 0

    lax.fori_loop(0, 8, rotate_low, 0)
    inv_root = 1.0 / math.sqrt(NMP * UNITS)

    def rotate_high(i, _):
        rows = pl.ds(pl.multiple_of(i * 16, 16), 16)
        rot[:, rows, :] = (butterfly(mid[:, rows, :]) * inv_root).astype(BF16)
        return 0

    lax.fori_loop(0, 4, rotate_high, 0)

    def give_back(j, to_y, first):
        def one(i, _):
            to_z = lax.rem(z + i, NZ)
            dest = to_z * NY + to_y
            send(rot.at[dest], recv2.at[j, z], a2_send.at[j], a2_recv.at[j], (dest, t))
            return 0

        lax.fori_loop(first, NZ, one, 0)

    def given(j):
        drain(rot.at[pl.ds(0, NZ if j < 3 else NZ - 1)], a2_send.at[j])

    give_back(0, ymod(y + 2), 0)
    recv2[3, z] = rot[m]

    def gather_own(j):
        count = NZ if j < 3 else NZ - 1
        drain(recv2.at[j, pl.ds(0, count)], a2_recv.at[j])

        def one(i, _):
            pieces = []
            for half in range(2):
                tall = recv2[j, 2 * i + half].astype(F32)
                pieces.append(
                    jnp.concatenate([tall[k * 8:k * 8 + 8] for k in range(8)], axis=1)
                )
            rows = pl.ds(pl.multiple_of(i * 16, 16), 16)
            act[j, t, rows, :] = jnp.concatenate(pieces, axis=0).astype(BF16)
            return 0

        lax.fori_loop(0, 4, one, 0)
        mine = act.at[j, t]
        for i in (1, 2, 3):
            dx = x_step(i)
            send(mine, mine, ag_send.at[j], ag_direct.at[j, i], at_x(lax.rem(x + dx, NX), core))
        send(mine, mine, ag_send.at[j], ag_core.at[j, 0], sibling)

    def x_step(i):
        return (0, 1, 3, 2)[i] if isinstance(i, int) else lax.rem(2 * i + 1, 3) + 1

    def chip_from(i):
        return lax.rem(x - x_step(i) + NX, NX)

    def pass_on(j, i):
        piece = act.at[j, chip_from(i) * 2 + core]
        drain(piece, ag_direct.at[j, i])
        send(piece, piece, ag_send.at[j], ag_core.at[j, i], sibling)

    def multiply(j, i, chip):
        drain(act.at[j, 0], ag_core.at[j, i])
        both = pl.ds(chip * 2, 2)
        part[j, both] = jnp.dot(
            act[j, both].reshape(2 * ROWS, UNITS), w[...], preferred_element_type=F32
        ).reshape(2, ROWS, COLS)

    def compose(d, step, j, zz, low, cut, incoming, dst):
        this, other = d * cut[0], (1 - d) * cut[0]
        if step == 1:
            dst[...] = part[j, zz, :, pl.ds(low + this, cut[d])].astype(BF16)
        elif step == 2:
            dst[:, pl.ds(this, cut[d])] = (
                part[j, zz, :, pl.ds(low + this, cut[d])] + incoming[...].astype(F32)
            ).astype(BF16)
            dst[:, pl.ds(other, cut[1 - d])] = (
                part[j, zz, :, pl.ds(low + other, cut[1 - d])].astype(BF16)
            )
        else:
            dst[...] = (
                part[j, zz, :, pl.ds(low, sum(cut))] + incoming[...].astype(F32)
            ).astype(BF16)

    def z_target(d, step):
        return zmod(z + (5 - step) * (1 - 2 * d))

    def z_hop(j, step, low, cut, s1, r1, s2, r2, s_sem, r1_sem, r2_sem):
        for d in range(2):
            zz = z_target(d, step)
            if step == 1:
                compose(d, 1, j, zz, low, cut, None, s1[d])
                send(s1[d], r1[d], s_sem.at[d], r1_sem.at[d], z_next[d])
                continue
            if step == 2:
                incoming, sem = r1[d], r1_sem.at[d]
            else:
                incoming, sem = r2.at[d, step - 3], r2_sem.at[d, step - 3]
            drain(incoming, sem)
            compose(d, step, j, zz, low, cut, incoming, s2.at[d, step - 2])
            send(
                s2.at[d, step - 2], r2.at[d, step - 2],
                s_sem.at[2], r2_sem.at[d, step - 2], z_next[d],
            )

    def z_first(j, step):
        z_hop(
            j, step, YW, Z_CUT, [b.at[j] for b in zs1], [b.at[j] for b in zr1],
            zs2.at[j], zr2.at[j],
            z_send, zr1_sem.at[j], zr2_sem.at[j],
        )

    def z_first_end(j):
        for d in range(2):
            drain(zr2.at[j, d, 2], zr2_sem.at[j, d, 2])
        part[j, z, :, pl.ds(YW, ZW)] = (
            part[j, z, :, pl.ds(YW, ZW)] + zr2[j, 0, 2].astype(F32) + zr2[j, 1, 2].astype(F32)
        )

    def z_second(step):
        z_hop(3, step, 0, Y_CUT, us1, ur1, us2, ur2, u_send, ur1_sem, ur2_sem)

    def block_at(k):
        up = lax.div(k + 1, 2)
        return zmod(z + 4 + up * (1 - 2 * lax.rem(k + 1, 2)))

    def y_first_start(chip):
        for one in range(2):
            zz = chip * 2 + one
            for d in range(2):
                compose(d, 1, 0, zz, 0, Y_CUT, None, ys1[d].at[zz])
                send(ys1[d].at[zz], yr1[d].at[zz], y_send.at[d], yr1_sem.at[d, zz], y_next[d])

    def y_first_pass(zz):
        for d in range(2):
            drain(yr1[d].at[zz], yr1_sem.at[d, zz])
            compose(d, 2, 1 + d, zz, 0, Y_CUT, yr1[d].at[zz], ys2.at[d, zz])
            send(ys2.at[d, zz], yr2.at[d, zz], y_send.at[2], yr2_sem.at[d, zz], y_next[d])

    def y_first_other(k, _):
        zz = block_at(k)

        @pl.when(lax.div(zz, 2) != x)
        def _():
            y_first_pass(zz)

        return 0

    def y_first_end(k, _):
        zz = block_at(k)
        for d in range(2):
            drain(yr2.at[d, zz], yr2_sem.at[d, zz])
        part[3, zz, :, pl.ds(0, YW)] = (
            part[3, zz, :, pl.ds(0, YW)] + yr2[0, zz].astype(F32) + yr2[1, zz].astype(F32)
        )
        return 0

    def y_second_start():
        for d in range(2):
            compose(d, 1, 0, z, YW, Z_CUT, None, vs1[d])
            send(vs1[d], vr1[d], v_send.at[d], vr1_sem.at[d], y_next[d])

    def y_second_pass(d):
        drain(vr1[d], vr1_sem.at[d])
        compose(d, 2, 1 + d, z, YW, Z_CUT, vr1[d], vs2.at[d])
        send(vs2.at[d], vr2.at[d], v_send.at[2], vr2_sem.at[d], y_next[d])

    def own_chip(j, _):
        multiply(j, 0, x)
        return 0

    def first_part(i, _):
        multiply(0, i, chip_from(i))
        y_first_start(chip_from(i))

        @pl.when(i == 1)
        def _():
            pass_on(0, 3)

        return 0

    def later_part(j):
        def one(i, _):
            multiply(j, i, chip_from(i))
            return 0

        return one

    given(0)
    give_back(1, ymod(y - 1), 0)
    gather_own(0)
    given(1)
    give_back(2, ymod(y + 1), 0)
    own_chip(0, 0)
    y_first_start(x)
    gather_own(1)
    given(2)
    give_back(3, y, 1)
    own_chip(1, 0)
    pass_on(0, 1)
    pass_on(0, 2)
    gather_own(2)
    own_chip(2, 0)
    lax.fori_loop(1, 4, first_part, 0)
    z_first(0, 1)
    gather_own(3)
    y_first_pass(2 * x)
    pass_on(1, 1)
    pass_on(1, 2)
    y_first_pass(2 * x + 1)
    z_first(0, 2)
    pass_on(1, 3)
    own_chip(3, 0)
    lax.fori_loop(1, 4, later_part(1), 0)
    z_first(1, 1)
    z_first(0, 3)
    pass_on(2, 1)
    pass_on(2, 2)
    z_first(1, 2)
    z_first(0, 4)
    pass_on(2, 3)
    lax.fori_loop(1, 4, later_part(2), 0)
    z_first(2, 1)
    z_first(1, 3)
    lax.fori_loop(0, 4, y_first_other, 0)
    pass_on(3, 1)
    pass_on(3, 2)
    z_first(2, 2)
    z_first(1, 4)
    pass_on(3, 3)
    lax.fori_loop(1, 4, later_part(3), 0)
    z_first(3, 1)
    z_first_end(0)
    y_second_start()
    z_first(2, 3)
    lax.fori_loop(4, 8, y_first_other, 0)
    z_first(3, 2)
    z_first_end(1)
    z_first(2, 4)
    lax.fori_loop(0, 1, y_first_end, 0)
    z_second(1)
    y_second_pass(0)
    z_first(3, 3)
    z_first_end(2)
    y_second_pass(1)
    lax.fori_loop(1, 3, y_first_end, 0)
    z_second(2)
    z_first(3, 4)
    lax.fori_loop(3, 5, y_first_end, 0)
    z_second(3)
    z_first_end(3)
    lax.fori_loop(5, 7, y_first_end, 0)
    z_second(4)
    lax.fori_loop(7, 8, y_first_end, 0)

    scales = jnp.exp2(-expo[...].astype(F32))
    for d in range(2):
        drain(vr2.at[d], vr2_sem.at[d])
    total = part[3, z, :, pl.ds(YW, ZW)] + vr2[0].astype(F32) + vr2[1].astype(F32)
    out[:, YW:] = (res[:, YW:].astype(F32) + total * scales[:, YW:]).astype(BF16)
    for d in range(2):
        drain(ur2.at[d, 2], ur2_sem.at[d, 2])
    total = part[3, z, :, pl.ds(0, YW)] + ur2[0, 2].astype(F32) + ur2[1, 2].astype(F32)
    out[:, :YW] = (res[:, :YW].astype(F32) + total * scales[:, :YW]).astype(BF16)

    drain(slab.at[pl.ds(0, NMP - 1)], a1_sem.at[0])
    given(3)
    for j in range(4):
        drain(act.at[j, pl.ds(0, 7)], ag_send.at[j])
    for first, second, sems in (
        (ys1, ys2, y_send), (zs1, zs2, z_send), (us1, us2, u_send), (vs1, vs2, v_send),
    ):
        for buf, sem in ((first[0], sems.at[0]), (first[1], sems.at[1]), (second, sems.at[2])):
            drain(buf, sem)


def per_device(hidden, sign_bits, down_weight, exponents, residual):
    vmem = pl.BlockSpec(memory_space=pltpu.VMEM)

    def pair(*shape):
        return [pltpu.VMEM(shape, BF16)] * 2

    def split(shape, cut):
        return [pltpu.VMEM(shape + (width,), BF16) for width in cut] * 2

    dma = pltpu.SemaphoreType.DMA
    return pl.pallas_call(
        kernel,
        out_shape=jax.ShapeDtypeStruct((ROWS, COLS), BF16),
        in_specs=[vmem, vmem, pl.BlockSpec(memory_space=pl.ANY), vmem, vmem],
        out_specs=vmem,
        scratch_shapes=[
            pltpu.VMEM((NMP, ROWS, LANES), BF16),
            pltpu.VMEM((NMP, ROWS, LANES), BF16),
            pltpu.VMEM((NMP, ROWS, LANES), F32),
            pltpu.VMEM((NMP, ROWS, LANES), BF16),
            pltpu.VMEM((4, NZ, ROWS, LANES), BF16),
            pltpu.VMEM((4, NZ, ROWS, UNITS), BF16),
            pltpu.VMEM((UNITS, COLS), BF16),
            pltpu.VMEM((UNITS, COLS), jnp.int32),
            pltpu.VMEM((4, NZ, ROWS, COLS), F32),
            *split((8, ROWS), Y_CUT), *pair(2, 8, ROWS, YW),
            *split((4, ROWS), Z_CUT), *pair(4, 2, 3, ROWS, ZW),
            *split((ROWS,), Y_CUT), *pair(2, 3, ROWS, YW),
            *split((ROWS,), Z_CUT), *pair(2, ROWS, ZW),
            dma((8,)), dma((2,)), dma((4,)), dma((4,)), dma((4,)), dma((4, 4)), dma((4, 4)),
            dma((3,)), dma((2, 8)), dma((2, 8)), dma((3,)), dma((4, 2)), dma((4, 2, 3)),
            dma((3,)), dma((2,)), dma((2, 3)), dma((3,)), dma((2,)), dma((2,)),
        ],
        compiler_params=pltpu.CompilerParams(
            collective_id=0, has_side_effects=True, vmem_limit_bytes=60 * 2**20
        ),
        cost_estimate=pl.CostEstimate(
            flops=2 * 2048 * UNITS * COLS, bytes_accessed=10 * 2**20, transcendentals=0
        ),
    )(
        hidden,
        sign_bits.reshape(1, UNITS),
        down_weight,
        exponents.reshape(1, COLS),
        residual,
    )


def solution(mesh):
    return jax.shard_map(
        per_device,
        mesh=mesh,
        in_specs=(P("tok", "mp"), P("mp"), P("mp", "tok"), P("tok"), P("mp", "tok")),
        out_specs=P("mp", "tok"),
        check_vma=False,
    )
```

```python
import functools
import math

import jax
import jax.numpy as jnp
from jax import lax
from jax.experimental import pallas as pl
from jax.experimental.pallas import tpu as pltpu
from jax.sharding import PartitionSpec as P

MESH = pl.DeviceIdType.MESH
F32, BF16 = jnp.float32, jnp.bfloat16
NZ, NY, NX = 8, 4, 4
NMP = NZ * NY
UNITS = 1024
LANES = 128
COLS = 2048
Y_CUT = (640, 640)
Z_CUT = (384, 384)
YW, ZW = sum(Y_CUT), sum(Z_CUT)
ROWS = 64


def butterfly(v):
    count = v.shape[0]
    rest = v.shape[1:]
    span = 1
    while span < count:
        pairs = v.reshape((count // (2 * span), 2, span) + rest)
        low, high = pairs[:, 0], pairs[:, 1]
        v = jnp.stack([low + high, low - high], axis=1).reshape((count,) + rest)
        span *= 2
    return v


def walsh(order):
    both = lax.broadcasted_iota(jnp.int32, (order, order), 0) & lax.broadcasted_iota(
        jnp.int32, (order, order), 1
    )
    both = both ^ (both >> 4)
    both = both ^ (both >> 2)
    both = both ^ (both >> 1)
    return (1 - 2 * (both & 1)).astype(F32).astype(BF16)


def send(src, dst, send_sem, recv_sem, device):
    pltpu.make_async_remote_copy(
        src_ref=src,
        dst_ref=dst,
        send_sem=send_sem,
        recv_sem=recv_sem,
        device_id=device,
        device_id_type=MESH,
    ).start()


def drain(buf, sem):
    pltpu.make_async_copy(buf, buf, sem).wait()


def kernel(
    hid, sgn, w_hbm, expo, res, out,
    slab, recv1, mid, rot, recv2, act, w, w32, part,
    ys1a, ys1b, yr1a, yr1b, ys2, yr2, zs1a, zs1b, zr1a, zr1b, zs2, zr2,
    us1a, us1b, ur1a, ur1b, us2, ur2, vs1a, vs1b, vr1a, vr1b, vs2, vr2,
    w_sem, a1_sem, a2_send, a2_recv, ag_send, ag_direct, ag_core,
    y_send, yr1_sem, yr2_sem, z_send, zr1_sem, zr2_sem,
    u_send, ur1_sem, ur2_sem, v_send, vr1_sem, vr2_sem,
):
    ys1, yr1, zs1, zr1 = (ys1a, ys1b), (yr1a, yr1b), (zs1a, zs1b), (zr1a, zr1b)
    us1, ur1, vs1, vr1 = (us1a, us1b), (ur1a, ur1b), (vs1a, vs1b), (vr1a, vr1b)
    m, t = lax.axis_index("mp"), lax.axis_index("tok")
    z, y = lax.div(m, NY), lax.rem(m, NY)
    x, core = lax.div(t, 2), lax.rem(t, 2)

    def zmod(v):
        return lax.rem(v + NZ, NZ)

    def ymod(v):
        return lax.rem(v + NY, NY)

    def at_zy(zz, yy):
        return (zz * NY + yy, t)

    def at_x(xx, cc):
        return (m, xx * 2 + cc)

    sibling = at_x(x, 1 - core)
    y_next = (at_zy(z, ymod(y + 1)), at_zy(z, ymod(y - 1)))
    z_next = (at_zy(zmod(z + 1), y), at_zy(zmod(z - 1), y))

    barrier = pltpu.get_barrier_semaphore()

    def far_first(i):
        offset = NMP // 2 + lax.div(i + 1, 2) * (1 - 2 * lax.rem(i, 2))
        return lax.rem(m + offset, NMP)

    def greet(i, _):
        pl.semaphore_signal(barrier, inc=1, device_id=(far_first(i), t), device_id_type=MESH)
        return 0

    lax.fori_loop(0, NMP - 1, greet, 0)
    for dx in (1, 2, 3):
        pl.semaphore_signal(
            barrier, inc=1, device_id=at_x(lax.rem(x + dx, NX), core), device_id_type=MESH
        )
    pl.semaphore_signal(barrier, inc=1, device_id=sibling, device_id_type=MESH)

    w_rows = UNITS // 8
    for i in range(8):
        rows = pl.ds(i * w_rows, w_rows)
        pltpu.make_async_copy(w_hbm.at[rows], w32.at[rows], w_sem.at[i]).start()

    signs = (2 * sgn[...] - 1).astype(F32)

    def build(j, _):
        rows = hid[pl.ds(pl.multiple_of(j * 16, 16), 16), :].astype(F32) * signs
        for half in range(2):
            group = 2 * j + half
            dest = lax.rem(group, NZ) * NY + lax.div(group, NZ)
            own = rows[half * 8:half * 8 + 8]
            tall = jnp.concatenate(
                [own[:, k * LANES:(k + 1) * LANES] for k in range(8)], axis=0
            )
            slab[dest] = tall.astype(BF16)
        return 0

    lax.fori_loop(0, 16, build, 0)
    pl.semaphore_wait(barrier, NMP - 1 + 4)

    def spread(i, _):
        dest = far_first(i)
        send(slab.at[dest], recv1.at[m], a1_sem.at[0], a1_sem.at[1], (dest, t))
        return 0

    lax.fori_loop(0, NMP - 1, spread, 0)
    recv1[m] = slab[m]

    def convert(j, _):
        rows = pl.ds(pl.multiple_of(j * 16, 16), 16)
        w[rows, :] = w32[rows, :].astype(F32).astype(BF16)
        return 0

    for i in range(8):
        rows = pl.ds(i * w_rows, w_rows)
        pltpu.make_async_copy(w_hbm.at[rows], w32.at[rows], w_sem.at[i]).wait()
        lax.fori_loop(i * w_rows // 16, (i + 1) * w_rows // 16, convert, 0)
    small_walsh = walsh(LANES)

    drain(recv1.at[pl.ds(0, NMP - 1)], a1_sem.at[1])

    def rotate_low(i, _):
        blocks = pl.ds(i * 4, 4)
        lanes = jnp.dot(
            recv1[blocks].reshape(256, LANES), small_walsh, preferred_element_type=F32
        ).reshape(4, 8, 8, LANES)
        for b in range(4):
            mid[i * 4 + b] = butterfly(lanes[b]).reshape(ROWS, LANES)
        return 0

    lax.fori_loop(0, 8, rotate_low, 0)
    inv_root = 1.0 / math.sqrt(NMP * UNITS)

    def rotate_high(i, _):
        rows = pl.ds(pl.multiple_of(i * 16, 16), 16)
        rot[:, rows, :] = (butterfly(mid[:, rows, :]) * inv_root).astype(BF16)
        return 0

    lax.fori_loop(0, 4, rotate_high, 0)

    def give_back(j, to_y, first):
        def one(i, _):
            to_z = lax.rem(z + i, NZ)
            dest = to_z * NY + to_y
            send(rot.at[dest], recv2.at[j, z], a2_send.at[j], a2_recv.at[j], (dest, t))
            return 0

        lax.fori_loop(first, NZ, one, 0)

    def given(j):
        drain(rot.at[pl.ds(0, NZ if j < 3 else NZ - 1)], a2_send.at[j])

    give_back(0, ymod(y + 2), 0)
    recv2[3, z] = rot[m]

    def gather_own(j):
        count = NZ if j < 3 else NZ - 1
        drain(recv2.at[j, pl.ds(0, count)], a2_recv.at[j])

        def one(i, _):
            pieces = []
            for half in range(2):
                tall = recv2[j, 2 * i + half].astype(F32)
                pieces.append(
                    jnp.concatenate([tall[k * 8:k * 8 + 8] for k in range(8)], axis=1)
                )
            rows = pl.ds(pl.multiple_of(i * 16, 16), 16)
            act[j, t, rows, :] = jnp.concatenate(pieces, axis=0).astype(BF16)
            return 0

        lax.fori_loop(0, 4, one, 0)
        mine = act.at[j, t]
        for i in (1, 2, 3):
            dx = x_step(i)
            send(mine, mine, ag_send.at[j], ag_direct.at[j, i], at_x(lax.rem(x + dx, NX), core))
        send(mine, mine, ag_send.at[j], ag_core.at[j, 0], sibling)

    def x_step(i):
        return (0, 1, 3, 2)[i] if isinstance(i, int) else lax.rem(2 * i + 1, 3) + 1

    def chip_from(i):
        return lax.rem(x - x_step(i) + NX, NX)

    def pass_on(j, i):
        piece = act.at[j, chip_from(i) * 2 + core]
        drain(piece, ag_direct.at[j, i])
        send(piece, piece, ag_send.at[j], ag_core.at[j, i], sibling)

    def multiply(j, i, chip):
        drain(act.at[j, 0], ag_core.at[j, i])
        both = pl.ds(chip * 2, 2)
        part[j, both] = jnp.dot(
            act[j, both].reshape(2 * ROWS, UNITS), w[...], preferred_element_type=F32
        ).reshape(2, ROWS, COLS)

    def compose(d, step, j, zz, low, cut, incoming, dst):
        this, other = d * cut[0], (1 - d) * cut[0]
        if step == 1:
            dst[...] = part[j, zz, :, pl.ds(low + this, cut[d])].astype(BF16)
        elif step == 2:
            dst[:, pl.ds(this, cut[d])] = (
                part[j, zz, :, pl.ds(low + this, cut[d])] + incoming[...].astype(F32)
            ).astype(BF16)
            dst[:, pl.ds(other, cut[1 - d])] = (
                part[j, zz, :, pl.ds(low + other, cut[1 - d])].astype(BF16)
            )
        else:
            dst[...] = (
                part[j, zz, :, pl.ds(low, sum(cut))] + incoming[...].astype(F32)
            ).astype(BF16)

    def z_target(d, step):
        return zmod(z + (5 - step) * (1 - 2 * d))

    def z_hop(j, step, low, cut, s1, r1, s2, r2, s_sem, r1_sem, r2_sem):
        for d in range(2):
            zz = z_target(d, step)
            if step == 1:
                compose(d, 1, j, zz, low, cut, None, s1[d])
                send(s1[d], r1[d], s_sem.at[d], r1_sem.at[d], z_next[d])
                continue
            if step == 2:
                incoming, sem = r1[d], r1_sem.at[d]
            else:
                incoming, sem = r2.at[d, step - 3], r2_sem.at[d, step - 3]
            drain(incoming, sem)
            compose(d, step, j, zz, low, cut, incoming, s2.at[d, step - 2])
            send(
                s2.at[d, step - 2], r2.at[d, step - 2],
                s_sem.at[2], r2_sem.at[d, step - 2], z_next[d],
            )

    def z_first(j, step):
        z_hop(
            j, step, YW, Z_CUT, [b.at[j] for b in zs1], [b.at[j] for b in zr1],
            zs2.at[j], zr2.at[j],
            z_send, zr1_sem.at[j], zr2_sem.at[j],
        )

    def z_first_end(j):
        for d in range(2):
            drain(zr2.at[j, d, 2], zr2_sem.at[j, d, 2])
        part[j, z, :, pl.ds(YW, ZW)] = (
            part[j, z, :, pl.ds(YW, ZW)] + zr2[j, 0, 2].astype(F32) + zr2[j, 1, 2].astype(F32)
        )

    def z_second(step):
        z_hop(3, step, 0, Y_CUT, us1, ur1, us2, ur2, u_send, ur1_sem, ur2_sem)

    def block_at(k):
        up = lax.div(k + 1, 2)
        return zmod(z + 4 + up * (1 - 2 * lax.rem(k + 1, 2)))

    def y_first_start(chip):
        for one in range(2):
            zz = chip * 2 + one
            for d in range(2):
                compose(d, 1, 0, zz, 0, Y_CUT, None, ys1[d].at[zz])
                send(ys1[d].at[zz], yr1[d].at[zz], y_send.at[d], yr1_sem.at[d, zz], y_next[d])

    def y_first_pass(zz):
        for d in range(2):
            drain(yr1[d].at[zz], yr1_sem.at[d, zz])
            compose(d, 2, 1 + d, zz, 0, Y_CUT, yr1[d].at[zz], ys2.at[d, zz])
            send(ys2.at[d, zz], yr2.at[d, zz], y_send.at[2], yr2_sem.at[d, zz], y_next[d])

    def y_first_other(k, _):
        zz = block_at(k)

        @pl.when(lax.div(zz, 2) != x)
        def _():
            y_first_pass(zz)

        return 0

    def y_first_end(k, _):
        zz = block_at(k)
        for d in range(2):
            drain(yr2.at[d, zz], yr2_sem.at[d, zz])
        part[3, zz, :, pl.ds(0, YW)] = (
            part[3, zz, :, pl.ds(0, YW)] + yr2[0, zz].astype(F32) + yr2[1, zz].astype(F32)
        )
        return 0

    def y_second_start():
        for d in range(2):
            compose(d, 1, 0, z, YW, Z_CUT, None, vs1[d])
            send(vs1[d], vr1[d], v_send.at[d], vr1_sem.at[d], y_next[d])

    def y_second_pass(d):
        drain(vr1[d], vr1_sem.at[d])
        compose(d, 2, 1 + d, z, YW, Z_CUT, vr1[d], vs2.at[d])
        send(vs2.at[d], vr2.at[d], v_send.at[2], vr2_sem.at[d], y_next[d])

    def own_chip(j, _):
        multiply(j, 0, x)
        return 0

    def first_part(i, _):
        multiply(0, i, chip_from(i))
        y_first_start(chip_from(i))

        @pl.when(i == 1)
        def _():
            pass_on(0, 3)

        return 0

    def later_part(j):
        def one(i, _):
            multiply(j, i, chip_from(i))
            return 0

        return one

    given(0)
    give_back(1, ymod(y - 1), 0)
    gather_own(0)
    given(1)
    give_back(2, ymod(y + 1), 0)
    own_chip(0, 0)
    y_first_start(x)
    gather_own(1)
    given(2)
    give_back(3, y, 1)
    own_chip(1, 0)
    pass_on(0, 1)
    pass_on(0, 2)
    gather_own(2)
    own_chip(2, 0)
    lax.fori_loop(1, 4, first_part, 0)
    z_first(0, 1)
    gather_own(3)
    y_first_pass(2 * x)
    pass_on(1, 1)
    pass_on(1, 2)
    y_first_pass(2 * x + 1)
    z_first(0, 2)
    pass_on(1, 3)
    own_chip(3, 0)
    lax.fori_loop(1, 4, later_part(1), 0)
    z_first(1, 1)
    z_first(0, 3)
    pass_on(2, 1)
    pass_on(2, 2)
    z_first(1, 2)
    z_first(0, 4)
    pass_on(2, 3)
    lax.fori_loop(1, 4, later_part(2), 0)
    z_first(2, 1)
    z_first(1, 3)
    lax.fori_loop(0, 2, y_first_other, 0)
    pass_on(3, 1)
    pass_on(3, 2)
    z_first(2, 2)
    z_first(1, 4)
    pass_on(3, 3)
    lax.fori_loop(1, 4, later_part(3), 0)
    z_first(3, 1)
    z_first(2, 3)
    z_first_end(0)
    lax.fori_loop(2, 4, y_first_other, 0)
    y_second_start()
    z_first(3, 2)
    z_first(2, 4)
    z_first_end(1)
    lax.fori_loop(0, 1, y_first_end, 0)
    z_second(1)
    lax.fori_loop(4, 5, y_first_other, 0)
    z_first(3, 3)
    z_first_end(2)
    lax.fori_loop(1, 3, y_first_end, 0)
    z_second(2)
    lax.fori_loop(5, 7, y_first_other, 0)
    z_first(3, 4)
    lax.fori_loop(3, 5, y_first_end, 0)
    z_second(3)
    lax.fori_loop(7, 8, y_first_other, 0)
    y_second_pass(0)
    y_second_pass(1)
    lax.fori_loop(5, 7, y_first_end, 0)
    z_second(4)
    z_first_end(3)
    lax.fori_loop(7, 8, y_first_end, 0)

    scales = jnp.exp2(-expo[...].astype(F32))
    for d in range(2):
        drain(vr2.at[d], vr2_sem.at[d])
    total = part[3, z, :, pl.ds(YW, ZW)] + vr2[0].astype(F32) + vr2[1].astype(F32)
    out[:, YW:] = (res[:, YW:].astype(F32) + total * scales[:, YW:]).astype(BF16)
    for d in range(2):
        drain(ur2.at[d, 2], ur2_sem.at[d, 2])
    total = part[3, z, :, pl.ds(0, YW)] + ur2[0, 2].astype(F32) + ur2[1, 2].astype(F32)
    out[:, :YW] = (res[:, :YW].astype(F32) + total * scales[:, :YW]).astype(BF16)

    drain(slab.at[pl.ds(0, NMP - 1)], a1_sem.at[0])
    given(3)
    for j in range(4):
        drain(act.at[j, pl.ds(0, 7)], ag_send.at[j])
    for first, second, sems in (
        (ys1, ys2, y_send), (zs1, zs2, z_send), (us1, us2, u_send), (vs1, vs2, v_send),
    ):
        for buf, sem in ((first[0], sems.at[0]), (first[1], sems.at[1]), (second, sems.at[2])):
            drain(buf, sem)


def per_device(hidden, sign_bits, down_weight, exponents, residual):
    vmem = pl.BlockSpec(memory_space=pltpu.VMEM)

    def pair(*shape):
        return [pltpu.VMEM(shape, BF16)] * 2

    def split(shape, cut):
        return [pltpu.VMEM(shape + (width,), BF16) for width in cut] * 2

    dma = pltpu.SemaphoreType.DMA
    return pl.pallas_call(
        kernel,
        out_shape=jax.ShapeDtypeStruct((ROWS, COLS), BF16),
        in_specs=[vmem, vmem, pl.BlockSpec(memory_space=pl.ANY), vmem, vmem],
        out_specs=vmem,
        scratch_shapes=[
            pltpu.VMEM((NMP, ROWS, LANES), BF16),
            pltpu.VMEM((NMP, ROWS, LANES), BF16),
            pltpu.VMEM((NMP, ROWS, LANES), F32),
            pltpu.VMEM((NMP, ROWS, LANES), BF16),
            pltpu.VMEM((4, NZ, ROWS, LANES), BF16),
            pltpu.VMEM((4, NZ, ROWS, UNITS), BF16),
            pltpu.VMEM((UNITS, COLS), BF16),
            pltpu.VMEM((UNITS, COLS), jnp.int32),
            pltpu.VMEM((4, NZ, ROWS, COLS), F32),
            *split((8, ROWS), Y_CUT), *pair(2, 8, ROWS, YW),
            *split((4, ROWS), Z_CUT), *pair(4, 2, 3, ROWS, ZW),
            *split((ROWS,), Y_CUT), *pair(2, 3, ROWS, YW),
            *split((ROWS,), Z_CUT), *pair(2, ROWS, ZW),
            dma((8,)), dma((2,)), dma((4,)), dma((4,)), dma((4,)), dma((4, 4)), dma((4, 4)),
            dma((3,)), dma((2, 8)), dma((2, 8)), dma((3,)), dma((4, 2)), dma((4, 2, 3)),
            dma((3,)), dma((2,)), dma((2, 3)), dma((3,)), dma((2,)), dma((2,)),
        ],
        compiler_params=pltpu.CompilerParams(
            collective_id=0, has_side_effects=True, vmem_limit_bytes=60 * 2**20
        ),
        cost_estimate=pl.CostEstimate(
            flops=2 * 2048 * UNITS * COLS, bytes_accessed=10 * 2**20, transcendentals=0
        ),
    )(
        hidden,
        sign_bits.reshape(1, UNITS),
        down_weight,
        exponents.reshape(1, COLS),
        residual,
    )


def solution(mesh):
    return jax.shard_map(
        per_device,
        mesh=mesh,
        in_specs=(P("tok", "mp"), P("mp"), P("mp", "tok"), P("tok"), P("mp", "tok")),
        out_specs=P("mp", "tok"),
        check_vma=False,
    )
```

```python
import functools
import math

import jax
import jax.numpy as jnp
from jax import lax
from jax.experimental import pallas as pl
from jax.experimental.pallas import tpu as pltpu
from jax.sharding import PartitionSpec as P

MESH = pl.DeviceIdType.MESH
F32, BF16 = jnp.float32, jnp.bfloat16
NZ, NY, NX = 8, 4, 4
NMP = NZ * NY
UNITS = 1024
LANES = 128
COLS = 2048
Y_CUT = (640, 640)
Z_CUT = (384, 384)
YW, ZW = sum(Y_CUT), sum(Z_CUT)
ROWS = 64


def butterfly(v):
    count = v.shape[0]
    rest = v.shape[1:]
    span = 1
    while span < count:
        pairs = v.reshape((count // (2 * span), 2, span) + rest)
        low, high = pairs[:, 0], pairs[:, 1]
        v = jnp.stack([low + high, low - high], axis=1).reshape((count,) + rest)
        span *= 2
    return v


def walsh(order):
    both = lax.broadcasted_iota(jnp.int32, (order, order), 0) & lax.broadcasted_iota(
        jnp.int32, (order, order), 1
    )
    both = both ^ (both >> 4)
    both = both ^ (both >> 2)
    both = both ^ (both >> 1)
    return (1 - 2 * (both & 1)).astype(F32).astype(BF16)


def send(src, dst, send_sem, recv_sem, device):
    pltpu.make_async_remote_copy(
        src_ref=src,
        dst_ref=dst,
        send_sem=send_sem,
        recv_sem=recv_sem,
        device_id=device,
        device_id_type=MESH,
    ).start()


def drain(buf, sem):
    pltpu.make_async_copy(buf, buf, sem).wait()


def kernel(
    hid, sgn, w_hbm, expo, res, out,
    slab, recv1, mid, rot, recv2, act, w, w32, part,
    ys1a, ys1b, yr1a, yr1b, ys2, yr2, zs1a, zs1b, zr1a, zr1b, zs2, zr2,
    us1a, us1b, ur1a, ur1b, us2, ur2, vs1a, vs1b, vr1a, vr1b, vs2, vr2,
    w_sem, a1_sem, a2_send, a2_recv, ag_send, ag_direct, ag_far, ag_core,
    y_send, yr1_sem, yr2_sem, z_send, zr1_sem, zr2_sem,
    u_send, ur1_sem, ur2_sem, v_send, vr1_sem, vr2_sem,
):
    ys1, yr1, zs1, zr1 = (ys1a, ys1b), (yr1a, yr1b), (zs1a, zs1b), (zr1a, zr1b)
    us1, ur1, vs1, vr1 = (us1a, us1b), (ur1a, ur1b), (vs1a, vs1b), (vr1a, vr1b)
    m, t = lax.axis_index("mp"), lax.axis_index("tok")
    z, y = lax.div(m, NY), lax.rem(m, NY)
    x, core = lax.div(t, 2), lax.rem(t, 2)

    def zmod(v):
        return lax.rem(v + NZ, NZ)

    def ymod(v):
        return lax.rem(v + NY, NY)

    def at_zy(zz, yy):
        return (zz * NY + yy, t)

    def at_x(xx, cc):
        return (m, xx * 2 + cc)

    sibling = at_x(x, 1 - core)
    y_next = (at_zy(z, ymod(y + 1)), at_zy(z, ymod(y - 1)))
    x_next = (at_x(lax.rem(x + 1, NX), core), at_x(lax.rem(x + 3, NX), core))
    z_next = (at_zy(zmod(z + 1), y), at_zy(zmod(z - 1), y))

    barrier = pltpu.get_barrier_semaphore()

    def far_first(i):
        offset = NMP // 2 + lax.div(i + 1, 2) * (1 - 2 * lax.rem(i, 2))
        return lax.rem(m + offset, NMP)

    def greet(i, _):
        pl.semaphore_signal(barrier, inc=1, device_id=(far_first(i), t), device_id_type=MESH)
        return 0

    lax.fori_loop(0, NMP - 1, greet, 0)
    for dx in (1, 2, 3):
        pl.semaphore_signal(
            barrier, inc=1, device_id=at_x(lax.rem(x + dx, NX), core), device_id_type=MESH
        )
    pl.semaphore_signal(barrier, inc=1, device_id=sibling, device_id_type=MESH)

    w_rows = UNITS // 8
    for i in range(8):
        rows = pl.ds(i * w_rows, w_rows)
        pltpu.make_async_copy(w_hbm.at[rows], w32.at[rows], w_sem.at[i]).start()

    signs = (2 * sgn[...] - 1).astype(F32)

    def build(j, _):
        rows = hid[pl.ds(pl.multiple_of(j * 16, 16), 16), :].astype(F32) * signs
        for half in range(2):
            group = 2 * j + half
            dest = lax.rem(group, NZ) * NY + lax.div(group, NZ)
            own = rows[half * 8:half * 8 + 8]
            tall = jnp.concatenate(
                [own[:, k * LANES:(k + 1) * LANES] for k in range(8)], axis=0
            )
            slab[dest] = tall.astype(BF16)
        return 0

    lax.fori_loop(0, 16, build, 0)
    pl.semaphore_wait(barrier, NMP - 1 + 4)

    def spread(i, _):
        dest = far_first(i)
        send(slab.at[dest], recv1.at[m], a1_sem.at[0], a1_sem.at[1], (dest, t))
        return 0

    lax.fori_loop(0, NMP - 1, spread, 0)
    recv1[m] = slab[m]

    def convert(j, _):
        rows = pl.ds(pl.multiple_of(j * 16, 16), 16)
        w[rows, :] = w32[rows, :].astype(F32).astype(BF16)
        return 0

    for i in range(8):
        rows = pl.ds(i * w_rows, w_rows)
        pltpu.make_async_copy(w_hbm.at[rows], w32.at[rows], w_sem.at[i]).wait()
        lax.fori_loop(i * w_rows // 16, (i + 1) * w_rows // 16, convert, 0)
    small_walsh = walsh(LANES)

    drain(recv1.at[pl.ds(0, NMP - 1)], a1_sem.at[1])

    def rotate_low(i, _):
        blocks = pl.ds(i * 4, 4)
        lanes = jnp.dot(
            recv1[blocks].reshape(256, LANES), small_walsh, preferred_element_type=F32
        ).reshape(4, 8, 8, LANES)
        for b in range(4):
            mid[i * 4 + b] = butterfly(lanes[b]).reshape(ROWS, LANES)
        return 0

    lax.fori_loop(0, 8, rotate_low, 0)
    inv_root = 1.0 / math.sqrt(NMP * UNITS)

    def rotate_high(i, _):
        rows = pl.ds(pl.multiple_of(i * 16, 16), 16)
        rot[:, rows, :] = (butterfly(mid[:, rows, :]) * inv_root).astype(BF16)
        return 0

    lax.fori_loop(0, 4, rotate_high, 0)

    def give_back(j, to_y, first):
        def one(i, _):
            to_z = lax.rem(z + i, NZ)
            dest = to_z * NY + to_y
            send(rot.at[dest], recv2.at[j, z], a2_send.at[j], a2_recv.at[j], (dest, t))
            return 0

        lax.fori_loop(first, NZ, one, 0)

    def given(j):
        drain(rot.at[pl.ds(0, NZ if j < 3 else NZ - 1)], a2_send.at[j])

    give_back(0, ymod(y + 2), 0)
    recv2[3, z] = rot[m]

    def gather_own(j):
        count = NZ if j < 3 else NZ - 1
        drain(recv2.at[j, pl.ds(0, count)], a2_recv.at[j])

        def one(i, _):
            pieces = []
            for half in range(2):
                tall = recv2[j, 2 * i + half].astype(F32)
                pieces.append(
                    jnp.concatenate([tall[k * 8:k * 8 + 8] for k in range(8)], axis=1)
                )
            rows = pl.ds(pl.multiple_of(i * 16, 16), 16)
            act[j, t, rows, :] = jnp.concatenate(pieces, axis=0).astype(BF16)
            return 0

        lax.fori_loop(0, 4, one, 0)
        mine = act.at[j, t]
        for i in (1, 2):
            send(mine, mine, ag_send.at[j], ag_direct.at[j, i], x_next[i - 1])
        send(mine, mine, ag_send.at[j], ag_core.at[j, 0], sibling)

    def x_step(i):
        return (0, 1, 3, 2)[i] if isinstance(i, int) else lax.rem(2 * i + 1, 3) + 1

    def chip_from(i):
        return lax.rem(x - x_step(i) + NX, NX)

    def pass_on(j, i):
        source = chip_from(i) * 2 + core
        piece = act.at[j, source]
        halves = [act.at[j, source, pl.ds(0, ROWS // 2)], act.at[j, source, pl.ds(ROWS // 2, ROWS // 2)]]
        if i < 3:
            drain(piece, ag_direct.at[j, i])
            half = halves[i - 1]
            send(half, half, ag_send.at[j], ag_far.at[j, i - 1], x_next[i - 1])
        else:
            for one in range(2):
                drain(halves[one], ag_far.at[j, one])
        send(piece, piece, ag_send.at[j], ag_core.at[j, i], sibling)

    def multiply(j, i, chip):
        drain(act.at[j, 0], ag_core.at[j, i])
        both = pl.ds(chip * 2, 2)
        part[j, both] = jnp.dot(
            act[j, both].reshape(2 * ROWS, UNITS), w[...], preferred_element_type=F32
        ).reshape(2, ROWS, COLS)

    def compose(d, step, j, zz, low, cut, incoming, dst):
        this, other = d * cut[0], (1 - d) * cut[0]
        if step == 1:
            dst[...] = part[j, zz, :, pl.ds(low + this, cut[d])].astype(BF16)
        elif step == 2:
            dst[:, pl.ds(this, cut[d])] = (
                part[j, zz, :, pl.ds(low + this, cut[d])] + incoming[...].astype(F32)
            ).astype(BF16)
            dst[:, pl.ds(other, cut[1 - d])] = (
                part[j, zz, :, pl.ds(low + other, cut[1 - d])].astype(BF16)
            )
        else:
            dst[...] = (
                part[j, zz, :, pl.ds(low, sum(cut))] + incoming[...].astype(F32)
            ).astype(BF16)

    def z_target(d, step):
        return zmod(z + (5 - step) * (1 - 2 * d))

    def z_hop(j, step, low, cut, s1, r1, s2, r2, s_sem, r1_sem, r2_sem):
        for d in range(2):
            zz = z_target(d, step)
            if step == 1:
                compose(d, 1, j, zz, low, cut, None, s1[d])
                send(s1[d], r1[d], s_sem.at[d], r1_sem.at[d], z_next[d])
                continue
            if step == 2:
                incoming, sem = r1[d], r1_sem.at[d]
            else:
                incoming, sem = r2.at[d, step - 3], r2_sem.at[d, step - 3]
            drain(incoming, sem)
            compose(d, step, j, zz, low, cut, incoming, s2.at[d, step - 2])
            send(
                s2.at[d, step - 2], r2.at[d, step - 2],
                s_sem.at[2], r2_sem.at[d, step - 2], z_next[d],
            )

    def z_first(j, step):
        z_hop(
            j, step, YW, Z_CUT, [b.at[j] for b in zs1], [b.at[j] for b in zr1],
            zs2.at[j], zr2.at[j],
            z_send, zr1_sem.at[j], zr2_sem.at[j],
        )

    def z_first_end(j):
        for d in range(2):
            drain(zr2.at[j, d, 2], zr2_sem.at[j, d, 2])
        part[j, z, :, pl.ds(YW, ZW)] = (
            part[j, z, :, pl.ds(YW, ZW)] + zr2[j, 0, 2].astype(F32) + zr2[j, 1, 2].astype(F32)
        )

    def z_second(step):
        z_hop(3, step, 0, Y_CUT, us1, ur1, us2, ur2, u_send, ur1_sem, ur2_sem)

    def block_at(k):
        up = lax.div(k + 1, 2)
        return zmod(z + 4 + up * (1 - 2 * lax.rem(k + 1, 2)))

    def y_first_start(chip):
        for one in range(2):
            zz = chip * 2 + one
            for d in range(2):
                compose(d, 1, 0, zz, 0, Y_CUT, None, ys1[d].at[zz])
                send(ys1[d].at[zz], yr1[d].at[zz], y_send.at[d], yr1_sem.at[d, zz], y_next[d])

    def y_first_pass(zz):
        for d in range(2):
            drain(yr1[d].at[zz], yr1_sem.at[d, zz])
            compose(d, 2, 1 + d, zz, 0, Y_CUT, yr1[d].at[zz], ys2.at[d, zz])
            send(ys2.at[d, zz], yr2.at[d, zz], y_send.at[2], yr2_sem.at[d, zz], y_next[d])

    def y_first_other(k, _):
        zz = block_at(k)

        @pl.when(lax.div(zz, 2) != x)
        def _():
            y_first_pass(zz)

        return 0

    def y_first_end(k, _):
        zz = block_at(k)
        for d in range(2):
            drain(yr2.at[d, zz], yr2_sem.at[d, zz])
        part[3, zz, :, pl.ds(0, YW)] = (
            part[3, zz, :, pl.ds(0, YW)] + yr2[0, zz].astype(F32) + yr2[1, zz].astype(F32)
        )
        return 0

    def y_second_start():
        for d in range(2):
            compose(d, 1, 0, z, YW, Z_CUT, None, vs1[d])
            send(vs1[d], vr1[d], v_send.at[d], vr1_sem.at[d], y_next[d])

    def y_second_pass(d):
        drain(vr1[d], vr1_sem.at[d])
        compose(d, 2, 1 + d, z, YW, Z_CUT, vr1[d], vs2.at[d])
        send(vs2.at[d], vr2.at[d], v_send.at[2], vr2_sem.at[d], y_next[d])

    def own_chip(j, _):
        multiply(j, 0, x)
        return 0

    def first_part(i, _):
        multiply(0, i, chip_from(i))
        y_first_start(chip_from(i))

        @pl.when(i == 1)
        def _():
            pass_on(0, 3)

        return 0

    def later_part(j):
        def one(i, _):
            multiply(j, i, chip_from(i))
            return 0

        return one

    given(0)
    give_back(1, ymod(y - 1), 0)
    gather_own(0)
    given(1)
    give_back(2, ymod(y + 1), 0)
    own_chip(0, 0)
    y_first_start(x)
    gather_own(1)
    given(2)
    give_back(3, y, 1)
    own_chip(1, 0)
    pass_on(0, 1)
    pass_on(0, 2)
    gather_own(2)
    own_chip(2, 0)
    lax.fori_loop(1, 4, first_part, 0)
    z_first(0, 1)
    gather_own(3)
    y_first_pass(2 * x)
    pass_on(1, 1)
    pass_on(1, 2)
    y_first_pass(2 * x + 1)
    z_first(0, 2)
    pass_on(1, 3)
    own_chip(3, 0)
    lax.fori_loop(1, 4, later_part(1), 0)
    z_first(1, 1)
    z_first(0, 3)
    pass_on(2, 1)
    pass_on(2, 2)
    z_first(1, 2)
    z_first(0, 4)
    pass_on(2, 3)
    lax.fori_loop(1, 4, later_part(2), 0)
    z_first(2, 1)
    z_first(1, 3)
    lax.fori_loop(0, 2, y_first_other, 0)
    pass_on(3, 1)
    pass_on(3, 2)
    z_first(2, 2)
    z_first(1, 4)
    pass_on(3, 3)
    lax.fori_loop(1, 4, later_part(3), 0)
    z_first(3, 1)
    z_first(2, 3)
    z_first_end(0)
    lax.fori_loop(2, 4, y_first_other, 0)
    y_second_start()
    z_first(3, 2)
    z_first(2, 4)
    z_first_end(1)
    lax.fori_loop(0, 1, y_first_end, 0)
    z_second(1)
    lax.fori_loop(4, 5, y_first_other, 0)
    z_first(3, 3)
    z_first_end(2)
    lax.fori_loop(1, 3, y_first_end, 0)
    z_second(2)
    lax.fori_loop(5, 7, y_first_other, 0)
    z_first(3, 4)
    lax.fori_loop(3, 5, y_first_end, 0)
    z_second(3)
    lax.fori_loop(7, 8, y_first_other, 0)
    y_second_pass(0)
    y_second_pass(1)
    lax.fori_loop(5, 7, y_first_end, 0)
    z_second(4)
    z_first_end(3)
    lax.fori_loop(7, 8, y_first_end, 0)

    scales = jnp.exp2(-expo[...].astype(F32))
    for d in range(2):
        drain(vr2.at[d], vr2_sem.at[d])
    total = part[3, z, :, pl.ds(YW, ZW)] + vr2[0].astype(F32) + vr2[1].astype(F32)
    out[:, YW:] = (res[:, YW:].astype(F32) + total * scales[:, YW:]).astype(BF16)
    for d in range(2):
        drain(ur2.at[d, 2], ur2_sem.at[d, 2])
    total = part[3, z, :, pl.ds(0, YW)] + ur2[0, 2].astype(F32) + ur2[1, 2].astype(F32)
    out[:, :YW] = (res[:, :YW].astype(F32) + total * scales[:, :YW]).astype(BF16)

    drain(slab.at[pl.ds(0, NMP - 1)], a1_sem.at[0])
    given(3)
    for j in range(4):
        drain(act.at[j, pl.ds(0, 7)], ag_send.at[j])
    for first, second, sems in (
        (ys1, ys2, y_send), (zs1, zs2, z_send), (us1, us2, u_send), (vs1, vs2, v_send),
    ):
        for buf, sem in ((first[0], sems.at[0]), (first[1], sems.at[1]), (second, sems.at[2])):
            drain(buf, sem)


def per_device(hidden, sign_bits, down_weight, exponents, residual):
    vmem = pl.BlockSpec(memory_space=pltpu.VMEM)

    def pair(*shape):
        return [pltpu.VMEM(shape, BF16)] * 2

    def split(shape, cut):
        return [pltpu.VMEM(shape + (width,), BF16) for width in cut] * 2

    dma = pltpu.SemaphoreType.DMA
    return pl.pallas_call(
        kernel,
        out_shape=jax.ShapeDtypeStruct((ROWS, COLS), BF16),
        in_specs=[vmem, vmem, pl.BlockSpec(memory_space=pl.ANY), vmem, vmem],
        out_specs=vmem,
        scratch_shapes=[
            pltpu.VMEM((NMP, ROWS, LANES), BF16),
            pltpu.VMEM((NMP, ROWS, LANES), BF16),
            pltpu.VMEM((NMP, ROWS, LANES), F32),
            pltpu.VMEM((NMP, ROWS, LANES), BF16),
            pltpu.VMEM((4, NZ, ROWS, LANES), BF16),
            pltpu.VMEM((4, NZ, ROWS, UNITS), BF16),
            pltpu.VMEM((UNITS, COLS), BF16),
            pltpu.VMEM((UNITS, COLS), jnp.int32),
            pltpu.VMEM((4, NZ, ROWS, COLS), F32),
            *split((8, ROWS), Y_CUT), *pair(2, 8, ROWS, YW),
            *split((4, ROWS), Z_CUT), *pair(4, 2, 3, ROWS, ZW),
            *split((ROWS,), Y_CUT), *pair(2, 3, ROWS, YW),
            *split((ROWS,), Z_CUT), *pair(2, ROWS, ZW),
            dma((8,)), dma((2,)), dma((4,)), dma((4,)), dma((4,)), dma((4, 4)), dma((4, 2)), dma((4, 4)),
            dma((3,)), dma((2, 8)), dma((2, 8)), dma((3,)), dma((4, 2)), dma((4, 2, 3)),
            dma((3,)), dma((2,)), dma((2, 3)), dma((3,)), dma((2,)), dma((2,)),
        ],
        compiler_params=pltpu.CompilerParams(
            collective_id=0, has_side_effects=True, vmem_limit_bytes=60 * 2**20
        ),
        cost_estimate=pl.CostEstimate(
            flops=2 * 2048 * UNITS * COLS, bytes_accessed=10 * 2**20, transcendentals=0
        ),
    )(
        hidden,
        sign_bits.reshape(1, UNITS),
        down_weight,
        exponents.reshape(1, COLS),
        residual,
    )


def solution(mesh):
    return jax.shard_map(
        per_device,
        mesh=mesh,
        in_specs=(P("tok", "mp"), P("mp"), P("mp", "tok"), P("tok"), P("mp", "tok")),
        out_specs=P("mp", "tok"),
        check_vma=False,
    )
```

```python
import functools
import math

import jax
import jax.numpy as jnp
from jax import lax
from jax.experimental import pallas as pl
from jax.experimental.pallas import tpu as pltpu
from jax.sharding import PartitionSpec as P

MESH = pl.DeviceIdType.MESH
F32, BF16 = jnp.float32, jnp.bfloat16
NZ, NY, NX = 8, 4, 4
NMP = NZ * NY
UNITS = 1024
LANES = 128
COLS = 2048
Y_CUT = (640, 640)
Z_CUT = (384, 384)
YW, ZW = sum(Y_CUT), sum(Z_CUT)
ROWS = 64


def butterfly(v):
    count = v.shape[0]
    rest = v.shape[1:]
    span = 1
    while span < count:
        pairs = v.reshape((count // (2 * span), 2, span) + rest)
        low, high = pairs[:, 0], pairs[:, 1]
        v = jnp.stack([low + high, low - high], axis=1).reshape((count,) + rest)
        span *= 2
    return v


def walsh(order):
    both = lax.broadcasted_iota(jnp.int32, (order, order), 0) & lax.broadcasted_iota(
        jnp.int32, (order, order), 1
    )
    both = both ^ (both >> 4)
    both = both ^ (both >> 2)
    both = both ^ (both >> 1)
    return (1 - 2 * (both & 1)).astype(F32).astype(BF16)


def send(src, dst, send_sem, recv_sem, device):
    pltpu.make_async_remote_copy(
        src_ref=src,
        dst_ref=dst,
        send_sem=send_sem,
        recv_sem=recv_sem,
        device_id=device,
        device_id_type=MESH,
    ).start()


def drain(buf, sem):
    pltpu.make_async_copy(buf, buf, sem).wait()


def kernel(
    hid, sgn, w_hbm, expo, res, out,
    slab, recv1, mid, rot, recv2, act, w, w32, part,
    ys1a, ys1b, yr1a, yr1b, ys2, yr2, zs1a, zs1b, zr1a, zr1b, zs2, zr2,
    us1a, us1b, ur1a, ur1b, us2, ur2, vs1a, vs1b, vr1a, vr1b, vs2, vr2,
    ring_sem, w_sem, a1_sem, a2_send, a2_recv, ag_send, ag_direct, ag_core,
    y_send, yr1_sem, yr2_sem, z_send, zr1_sem, zr2_sem,
    u_send, ur1_sem, ur2_sem, v_send, vr1_sem, vr2_sem,
):
    ys1, yr1, zs1, zr1 = (ys1a, ys1b), (yr1a, yr1b), (zs1a, zs1b), (zr1a, zr1b)
    us1, ur1, vs1, vr1 = (us1a, us1b), (ur1a, ur1b), (vs1a, vs1b), (vr1a, vr1b)
    m, t = lax.axis_index("mp"), lax.axis_index("tok")
    z, y = lax.div(m, NY), lax.rem(m, NY)
    x, core = lax.div(t, 2), lax.rem(t, 2)

    def zmod(v):
        return lax.rem(v + NZ, NZ)

    def ymod(v):
        return lax.rem(v + NY, NY)

    def at_zy(zz, yy):
        return (zz * NY + yy, t)

    def at_x(xx, cc):
        return (m, xx * 2 + cc)

    sibling = at_x(x, 1 - core)
    y_next = (at_zy(z, ymod(y + 1)), at_zy(z, ymod(y - 1)))
    z_next = (at_zy(zmod(z + 1), y), at_zy(zmod(z - 1), y))

    barrier = pltpu.get_barrier_semaphore()

    def far_first(i):
        offset = NMP // 2 + lax.div(i + 1, 2) * (1 - 2 * lax.rem(i, 2))
        return lax.rem(m + offset, NMP)

    def greet(device):
        pl.semaphore_signal(barrier, inc=1, device_id=device, device_id_type=MESH)

    for dz in (4, 3, 5, 2, 6, 1, 7):
        greet(at_zy(zmod(z + dz), y))
    for dy in (2, 1, 3):
        greet(at_zy(z, ymod(y + dy)))
    for dx in (1, 2, 3):
        pl.semaphore_signal(
            barrier, inc=1, device_id=at_x(lax.rem(x + dx, NX), core), device_id_type=MESH
        )
    pl.semaphore_signal(barrier, inc=1, device_id=sibling, device_id_type=MESH)

    w_rows = UNITS // 8
    for i in range(8):
        rows = pl.ds(i * w_rows, w_rows)
        pltpu.make_async_copy(w_hbm.at[rows], w32.at[rows], w_sem.at[i]).start()

    signs = (2 * sgn[...] - 1).astype(F32)

    def build(j, _):
        rows = hid[pl.ds(pl.multiple_of(j * 16, 16), 16), :].astype(F32) * signs
        for half in range(2):
            group = 2 * j + half
            dest = lax.rem(group, NZ) * NY + lax.div(group, NZ)
            own = rows[half * 8:half * 8 + 8]
            tall = jnp.concatenate(
                [own[:, k * LANES:(k + 1) * LANES] for k in range(8)], axis=0
            )
            slab[dest] = tall.astype(BF16)
        return 0

    lax.fori_loop(0, 16, build, 0)
    pl.semaphore_wait(barrier, NZ - 1 + NY - 1 + 4)
    for dy in (2, 1, 3):
        pl.semaphore_signal(
            ring_sem, inc=1, device_id=at_zy(z, ymod(y + dy)), device_id_type=MESH
        )
    pl.semaphore_wait(ring_sem, NY - 1)

    def spread(i, _):
        dest = far_first(i)
        send(slab.at[dest], recv1.at[m], a1_sem.at[0], a1_sem.at[1], (dest, t))
        return 0

    lax.fori_loop(0, NMP - 1, spread, 0)
    recv1[m] = slab[m]

    def convert(j, _):
        rows = pl.ds(pl.multiple_of(j * 16, 16), 16)
        w[rows, :] = w32[rows, :].astype(F32).astype(BF16)
        return 0

    for i in range(8):
        rows = pl.ds(i * w_rows, w_rows)
        pltpu.make_async_copy(w_hbm.at[rows], w32.at[rows], w_sem.at[i]).wait()
        lax.fori_loop(i * w_rows // 16, (i + 1) * w_rows // 16, convert, 0)
    small_walsh = walsh(LANES)

    drain(recv1.at[pl.ds(0, NMP - 1)], a1_sem.at[1])

    def rotate_low(i, _):
        blocks = pl.ds(i * 4, 4)
        lanes = jnp.dot(
            recv1[blocks].reshape(256, LANES), small_walsh, preferred_element_type=F32
        ).reshape(4, 8, 8, LANES)
        for b in range(4):
            mid[i * 4 + b] = butterfly(lanes[b]).reshape(ROWS, LANES)
        return 0

    lax.fori_loop(0, 8, rotate_low, 0)
    inv_root = 1.0 / math.sqrt(NMP * UNITS)

    def rotate_high(i, _):
        rows = pl.ds(pl.multiple_of(i * 16, 16), 16)
        rot[:, rows, :] = (butterfly(mid[:, rows, :]) * inv_root).astype(BF16)
        return 0

    lax.fori_loop(0, 4, rotate_high, 0)

    def give_back(j, to_y, first):
        def one(i, _):
            to_z = lax.rem(z + i, NZ)
            dest = to_z * NY + to_y
            send(rot.at[dest], recv2.at[j, z], a2_send.at[j], a2_recv.at[j], (dest, t))
            return 0

        lax.fori_loop(first, NZ, one, 0)

    def given(j):
        drain(rot.at[pl.ds(0, NZ if j < 3 else NZ - 1)], a2_send.at[j])

    give_back(0, ymod(y + 2), 0)
    recv2[3, z] = rot[m]

    def gather_own(j):
        count = NZ if j < 3 else NZ - 1
        drain(recv2.at[j, pl.ds(0, count)], a2_recv.at[j])

        def one(i, _):
            pieces = []
            for half in range(2):
                tall = recv2[j, 2 * i + half].astype(F32)
                pieces.append(
                    jnp.concatenate([tall[k * 8:k * 8 + 8] for k in range(8)], axis=1)
                )
            rows = pl.ds(pl.multiple_of(i * 16, 16), 16)
            act[j, t, rows, :] = jnp.concatenate(pieces, axis=0).astype(BF16)
            return 0

        lax.fori_loop(0, 4, one, 0)
        mine = act.at[j, t]
        for i in (1, 2, 3):
            dx = x_step(i)
            send(mine, mine, ag_send.at[j], ag_direct.at[j, i], at_x(lax.rem(x + dx, NX), core))
        send(mine, mine, ag_send.at[j], ag_core.at[j, 0], sibling)

    def x_step(i):
        return (0, 1, 3, 2)[i] if isinstance(i, int) else lax.rem(2 * i + 1, 3) + 1

    def chip_from(i):
        return lax.rem(x - x_step(i) + NX, NX)

    def pass_on(j, i):
        piece = act.at[j, chip_from(i) * 2 + core]
        drain(piece, ag_direct.at[j, i])
        send(piece, piece, ag_send.at[j], ag_core.at[j, i], sibling)

    def multiply(j, i, chip):
        drain(act.at[j, 0], ag_core.at[j, i])
        both = pl.ds(chip * 2, 2)
        part[j, both] = jnp.dot(
            act[j, both].reshape(2 * ROWS, UNITS), w[...], preferred_element_type=F32
        ).reshape(2, ROWS, COLS)

    def compose(d, step, j, zz, low, cut, incoming, dst):
        this, other = d * cut[0], (1 - d) * cut[0]
        if step == 1:
            dst[...] = part[j, zz, :, pl.ds(low + this, cut[d])].astype(BF16)
        elif step == 2:
            dst[:, pl.ds(this, cut[d])] = (
                part[j, zz, :, pl.ds(low + this, cut[d])] + incoming[...].astype(F32)
            ).astype(BF16)
            dst[:, pl.ds(other, cut[1 - d])] = (
                part[j, zz, :, pl.ds(low + other, cut[1 - d])].astype(BF16)
            )
        else:
            dst[...] = (
                part[j, zz, :, pl.ds(low, sum(cut))] + incoming[...].astype(F32)
            ).astype(BF16)

    def z_target(d, step):
        return zmod(z + (5 - step) * (1 - 2 * d))

    def z_hop(j, step, low, cut, s1, r1, s2, r2, s_sem, r1_sem, r2_sem):
        for d in range(2):
            zz = z_target(d, step)
            if step == 1:
                compose(d, 1, j, zz, low, cut, None, s1[d])
                send(s1[d], r1[d], s_sem.at[d], r1_sem.at[d], z_next[d])
                continue
            if step == 2:
                incoming, sem = r1[d], r1_sem.at[d]
            else:
                incoming, sem = r2.at[d, step - 3], r2_sem.at[d, step - 3]
            drain(incoming, sem)
            compose(d, step, j, zz, low, cut, incoming, s2.at[d, step - 2])
            send(
                s2.at[d, step - 2], r2.at[d, step - 2],
                s_sem.at[2], r2_sem.at[d, step - 2], z_next[d],
            )

    def z_first(j, step):
        z_hop(
            j, step, YW, Z_CUT, [b.at[j] for b in zs1], [b.at[j] for b in zr1],
            zs2.at[j], zr2.at[j],
            z_send, zr1_sem.at[j], zr2_sem.at[j],
        )

    def z_first_end(j):
        for d in range(2):
            drain(zr2.at[j, d, 2], zr2_sem.at[j, d, 2])
        part[j, z, :, pl.ds(YW, ZW)] = (
            part[j, z, :, pl.ds(YW, ZW)] + zr2[j, 0, 2].astype(F32) + zr2[j, 1, 2].astype(F32)
        )

    def z_second(step):
        z_hop(3, step, 0, Y_CUT, us1, ur1, us2, ur2, u_send, ur1_sem, ur2_sem)

    def block_at(k):
        up = lax.div(k + 1, 2)
        return zmod(z + 4 + up * (1 - 2 * lax.rem(k + 1, 2)))

    def y_first_start(chip):
        for one in range(2):
            zz = chip * 2 + one
            for d in range(2):
                compose(d, 1, 0, zz, 0, Y_CUT, None, ys1[d].at[zz])
                send(ys1[d].at[zz], yr1[d].at[zz], y_send.at[d], yr1_sem.at[d, zz], y_next[d])

    def y_first_pass(zz):
        for d in range(2):
            drain(yr1[d].at[zz], yr1_sem.at[d, zz])
            compose(d, 2, 1 + d, zz, 0, Y_CUT, yr1[d].at[zz], ys2.at[d, zz])
            send(ys2.at[d, zz], yr2.at[d, zz], y_send.at[2], yr2_sem.at[d, zz], y_next[d])

    def y_first_other(k, _):
        zz = block_at(k)

        @pl.when(lax.div(zz, 2) != x)
        def _():
            y_first_pass(zz)

        return 0

    def y_first_end(k, _):
        zz = block_at(k)
        for d in range(2):
            drain(yr2.at[d, zz], yr2_sem.at[d, zz])
        part[3, zz, :, pl.ds(0, YW)] = (
            part[3, zz, :, pl.ds(0, YW)] + yr2[0, zz].astype(F32) + yr2[1, zz].astype(F32)
        )
        return 0

    def y_second_start():
        for d in range(2):
            compose(d, 1, 0, z, YW, Z_CUT, None, vs1[d])
            send(vs1[d], vr1[d], v_send.at[d], vr1_sem.at[d], y_next[d])

    def y_second_pass(d):
        drain(vr1[d], vr1_sem.at[d])
        compose(d, 2, 1 + d, z, YW, Z_CUT, vr1[d], vs2.at[d])
        send(vs2.at[d], vr2.at[d], v_send.at[2], vr2_sem.at[d], y_next[d])

    def own_chip(j, _):
        multiply(j, 0, x)
        return 0

    def first_part(i, _):
        multiply(0, i, chip_from(i))
        y_first_start(chip_from(i))

        @pl.when(i == 1)
        def _():
            pass_on(0, 3)

        return 0

    def later_part(j):
        def one(i, _):
            multiply(j, i, chip_from(i))
            return 0

        return one

    given(0)
    give_back(1, ymod(y - 1), 0)
    gather_own(0)
    given(1)
    give_back(2, ymod(y + 1), 0)
    own_chip(0, 0)
    y_first_start(x)
    gather_own(1)
    given(2)
    give_back(3, y, 1)
    own_chip(1, 0)
    pass_on(0, 1)
    pass_on(0, 2)
    gather_own(2)
    own_chip(2, 0)
    lax.fori_loop(1, 4, first_part, 0)
    z_first(0, 1)
    gather_own(3)
    y_first_pass(2 * x)
    pass_on(1, 1)
    pass_on(1, 2)
    y_first_pass(2 * x + 1)
    z_first(0, 2)
    pass_on(1, 3)
    own_chip(3, 0)
    lax.fori_loop(1, 4, later_part(1), 0)
    z_first(1, 1)
    z_first(0, 3)
    pass_on(2, 1)
    pass_on(2, 2)
    z_first(1, 2)
    z_first(0, 4)
    pass_on(2, 3)
    lax.fori_loop(1, 4, later_part(2), 0)
    z_first(2, 1)
    z_first(1, 3)
    lax.fori_loop(0, 2, y_first_other, 0)
    pass_on(3, 1)
    pass_on(3, 2)
    z_first(2, 2)
    z_first(1, 4)
    pass_on(3, 3)
    lax.fori_loop(1, 4, later_part(3), 0)
    z_first(3, 1)
    z_first(2, 3)
    z_first_end(0)
    lax.fori_loop(2, 4, y_first_other, 0)
    y_second_start()
    z_first(3, 2)
    z_first(2, 4)
    z_first_end(1)
    lax.fori_loop(0, 1, y_first_end, 0)
    z_second(1)
    lax.fori_loop(4, 5, y_first_other, 0)
    z_first(3, 3)
    z_first_end(2)
    lax.fori_loop(1, 3, y_first_end, 0)
    z_second(2)
    lax.fori_loop(5, 7, y_first_other, 0)
    z_first(3, 4)
    lax.fori_loop(3, 5, y_first_end, 0)
    z_second(3)
    lax.fori_loop(7, 8, y_first_other, 0)
    y_second_pass(0)
    y_second_pass(1)
    lax.fori_loop(5, 7, y_first_end, 0)
    z_second(4)
    z_first_end(3)
    lax.fori_loop(7, 8, y_first_end, 0)

    scales = jnp.exp2(-expo[...].astype(F32))
    for d in range(2):
        drain(vr2.at[d], vr2_sem.at[d])
    total = part[3, z, :, pl.ds(YW, ZW)] + vr2[0].astype(F32) + vr2[1].astype(F32)
    out[:, YW:] = (res[:, YW:].astype(F32) + total * scales[:, YW:]).astype(BF16)
    for d in range(2):
        drain(ur2.at[d, 2], ur2_sem.at[d, 2])
    total = part[3, z, :, pl.ds(0, YW)] + ur2[0, 2].astype(F32) + ur2[1, 2].astype(F32)
    out[:, :YW] = (res[:, :YW].astype(F32) + total * scales[:, :YW]).astype(BF16)

    drain(slab.at[pl.ds(0, NMP - 1)], a1_sem.at[0])
    given(3)
    for j in range(4):
        drain(act.at[j, pl.ds(0, 7)], ag_send.at[j])
    for first, second, sems in (
        (ys1, ys2, y_send), (zs1, zs2, z_send), (us1, us2, u_send), (vs1, vs2, v_send),
    ):
        for buf, sem in ((first[0], sems.at[0]), (first[1], sems.at[1]), (second, sems.at[2])):
            drain(buf, sem)


def per_device(hidden, sign_bits, down_weight, exponents, residual):
    vmem = pl.BlockSpec(memory_space=pltpu.VMEM)

    def pair(*shape):
        return [pltpu.VMEM(shape, BF16)] * 2

    def split(shape, cut):
        return [pltpu.VMEM(shape + (width,), BF16) for width in cut] * 2

    dma = pltpu.SemaphoreType.DMA
    return pl.pallas_call(
        kernel,
        out_shape=jax.ShapeDtypeStruct((ROWS, COLS), BF16),
        in_specs=[vmem, vmem, pl.BlockSpec(memory_space=pl.ANY), vmem, vmem],
        out_specs=vmem,
        scratch_shapes=[
            pltpu.VMEM((NMP, ROWS, LANES), BF16),
            pltpu.VMEM((NMP, ROWS, LANES), BF16),
            pltpu.VMEM((NMP, ROWS, LANES), F32),
            pltpu.VMEM((NMP, ROWS, LANES), BF16),
            pltpu.VMEM((4, NZ, ROWS, LANES), BF16),
            pltpu.VMEM((4, NZ, ROWS, UNITS), BF16),
            pltpu.VMEM((UNITS, COLS), BF16),
            pltpu.VMEM((UNITS, COLS), jnp.int32),
            pltpu.VMEM((4, NZ, ROWS, COLS), F32),
            *split((8, ROWS), Y_CUT), *pair(2, 8, ROWS, YW),
            *split((4, ROWS), Z_CUT), *pair(4, 2, 3, ROWS, ZW),
            *split((ROWS,), Y_CUT), *pair(2, 3, ROWS, YW),
            *split((ROWS,), Z_CUT), *pair(2, ROWS, ZW),
            pltpu.SemaphoreType.REGULAR,
            dma((8,)), dma((2,)), dma((4,)), dma((4,)), dma((4,)), dma((4, 4)), dma((4, 4)),
            dma((3,)), dma((2, 8)), dma((2, 8)), dma((3,)), dma((4, 2)), dma((4, 2, 3)),
            dma((3,)), dma((2,)), dma((2, 3)), dma((3,)), dma((2,)), dma((2,)),
        ],
        compiler_params=pltpu.CompilerParams(
            collective_id=0, has_side_effects=True, vmem_limit_bytes=60 * 2**20
        ),
        cost_estimate=pl.CostEstimate(
            flops=2 * 2048 * UNITS * COLS, bytes_accessed=10 * 2**20, transcendentals=0
        ),
    )(
        hidden,
        sign_bits.reshape(1, UNITS),
        down_weight,
        exponents.reshape(1, COLS),
        residual,
    )


def solution(mesh):
    return jax.shard_map(
        per_device,
        mesh=mesh,
        in_specs=(P("tok", "mp"), P("mp"), P("mp", "tok"), P("tok"), P("mp", "tok")),
        out_specs=P("mp", "tok"),
        check_vma=False,
    )
```
